32 devices in a mesh: lat: 4 (over y, core), lon: 8 (over z, x).
Axes of the slice: x: 2, y: 2, z: 4, core: 2. Of those that a mesh axis runs over, the one named last changes fastest.
Arguments:
- latent: bfloat16 [24, 2, 64, 640], P('lat', None, 'lon'), may hold values from -6 to 6
- norm_gain: float32 [640], replicated, may hold values from 0.25 to 1.75
- filters: bfloat16 [9, 24, 4, 8], P(None, 'lat'), may hold values from -1 to 1
- row_offsets: int32 [24, 4], P('lat'), may hold values from -2 to 2
- col_offsets: int32 [24, 4], P('lat'), may hold values from -6 to -2
- mix_weight: bfloat16 [9, 640, 640], P(None, 'lat', 'lon'), may hold values from -0.078125 to 0.078125
- up_weight: bfloat16 [640, 1280], P('lat', 'lon'), may hold values from -0.25 to 0.25
- up_bias: float32 [1280], replicated, may hold values from -3 to 3
- down_weight: bfloat16 [1280, 640], P('lat', 'lon'), may hold values from -0.15625 to 0.15625
Outputs:
- output: bfloat16 [24, 2, 64, 640], P('lat', None, 'lon')
The draws below stay inside these ranges and needn't reach their ends.
All inputs are finite; a program needn't handle non-finite values.
Results may differ from the reference program's by a relative error of at most 0.0059.
Values may be sent and summed in bfloat16 or wider, within the bound.
No kernel may reach another device: no remote copies, remote signals or barrier semaphores. Data moves between devices by JAX's collectives and lax.ppermute only.
A program may use at most 64 MiB of HBM per device.

```python
import jax
import jax.numpy as jnp
from jax import lax

C = 640
HID = 1280
KB = 9
E = 2
R = 4
BW = 8
HREACH = 2
NLAT = 24
NLON = 64


def with_ends(values, key, low, high):
    extent = values.shape
    spot = [jax.random.randint(jax.random.fold_in(key, axis), (), 0, extent[axis]) for axis in range(len(extent))]
    values = values.at[tuple(spot)].set(low)
    longest = extent.index(max(extent))
    spot[longest] = (spot[longest] + 1) % extent[longest]
    return values.at[tuple(spot)].set(high)


def block_levels(stream_key, shape, shards, smallest, high):
    factor_of = 1.0
    for position, parts in shards:
        steps = jax.random.uniform(jax.random.fold_in(jax.random.fold_in(stream_key, 6), position), (parts,), jnp.float32, smallest / len(shards), high / len(shards))
        factor_of = factor_of * jnp.repeat(jnp.exp(steps), shape[position] // parts).reshape((-1,) + (1,) * (len(shape) - 1 - position))
    return factor_of


def centred(rng, dims, width, reach, cuts=(), held_as=jnp.bfloat16):
    values = width * jax.random.normal(rng, dims, jnp.float32)
    if cuts:
        values = values * block_levels(rng, dims, cuts, -0.22, 0.18)
    return jnp.clip(values, -reach, reach).astype(held_as)


def setup_inputs(seed: int = 0) -> dict:
    seeds = jax.random.split(jax.random.key(seed), 10)
    latent = centred(seeds[0], (NLAT, E, NLON, C), 1.0, 6.0, ((0, 4), (2, 8)))
    norm_gain = jnp.clip(1.0 + 0.15 * jax.random.normal(seeds[1], (C,), jnp.float32), 0.25, 1.75)
    filters = centred(seeds[2], (KB, NLAT, R, BW), (R * BW) ** -0.5, 1.0, ((1, 4),))
    row_offsets = with_ends(jax.random.randint(seeds[3], (NLAT, R), 0 - HREACH, HREACH + 1), jax.random.fold_in(seeds[3], 1), 0 - HREACH, HREACH).astype(jnp.int32)
    col_offsets = with_ends(jax.random.randint(seeds[4], (NLAT, R), 0 - BW // 2 - 2, 3 - BW // 2), jax.random.fold_in(seeds[4], 1), 0 - BW // 2 - 2, (3 - BW // 2) - 1).astype(jnp.int32)
    mix_weight = centred(seeds[5], (KB, C, C), (KB * C) ** -0.5, 0.078125, ((1, 4), (2, 8)))
    up_weight = centred(seeds[6], (C, HID), C ** -0.5, 0.25, ((0, 4), (1, 8)))
    up_bias = centred(seeds[7], (HID,), 0.5, 3.0, (), jnp.float32)
    down_weight = centred(seeds[8], (HID, C), HID ** -0.5, 0.15625, ((0, 4), (1, 8)))
    return dict(latent=latent, norm_gain=norm_gain, filters=filters, row_offsets=row_offsets, col_offsets=col_offsets, mix_weight=mix_weight, up_weight=up_weight, up_bias=up_bias, down_weight=down_weight)


EPSILON = 1e-05

def normalize(latent, norm_gain):
    widened = latent.astype(jnp.float32)
    channel_mean = lax.optimization_barrier(jnp.mean(widened, axis=-1, keepdims=True))
    centered = widened - channel_mean
    variance = lax.optimization_barrier(jnp.mean(centered * centered, axis=-1, keepdims=True))
    return (centered * lax.rsqrt(variance + EPSILON) * norm_gain).astype(jnp.bfloat16)

def reference(latent, norm_gain, filters, row_offsets, col_offsets, mix_weight, up_weight, up_bias, down_weight):
    normalized = normalize(latent, norm_gain)
    padded = jnp.pad(normalized, ((HREACH, HREACH), (0, 0), (0, 0), (0, 0)))
    mixing = mix_weight.reshape(KB * C, C)

    def cycle_output(cycle_index):
        pieces = []
        for row_slot in range(R):
            where = cycle_index + HREACH + row_offsets[cycle_index, row_slot]
            source = lax.dynamic_index_in_dim(padded, where.astype(jnp.int32), 0, keepdims=False)
            tripled = jnp.concatenate([source, source, source[:, :BW]], axis=1)
            start = jnp.mod(col_offsets[cycle_index, row_slot], NLON).astype(jnp.int32)
            segment = lax.dynamic_slice_in_dim(tripled, start, NLON + BW, 1)
            for band_step in range(BW):
                pieces.append(segment[:, band_step:band_step + NLON])
        stacked = jnp.stack(pieces).reshape(R * BW, E * NLON * C)
        cycle_filter = lax.dynamic_index_in_dim(filters, cycle_index, 1, keepdims=False).reshape(KB, R * BW)
        contracted = jnp.dot(cycle_filter, stacked, preferred_element_type=jnp.float32).astype(jnp.bfloat16)
        regrouped = contracted.reshape(KB, E * NLON, C).transpose(1, 0, 2).reshape(E * NLON, KB * C)
        convolved = jnp.dot(regrouped, mixing, preferred_element_type=jnp.float32)
        own_cycle = lax.dynamic_index_in_dim(latent, cycle_index, 0, keepdims=False).reshape(E * NLON, C)
        hidden = (own_cycle.astype(jnp.float32) + convolved).astype(jnp.bfloat16)
        lifted = jnp.dot(hidden, up_weight, preferred_element_type=jnp.float32) + up_bias
        activated = jax.nn.gelu(lifted, approximate=False).astype(jnp.bfloat16)
        result = hidden.astype(jnp.float32) + jnp.dot(activated, down_weight, preferred_element_type=jnp.float32)
        return result.astype(jnp.bfloat16).reshape(E, NLON, C)
    return lax.map(cycle_output, jnp.arange(NLAT, dtype=jnp.int32))
```

```python
import jax
import jax.numpy as jnp
from jax import lax
from jax.experimental import pallas as pl
from jax.experimental.pallas import tpu as pltpu
from jax.sharding import PartitionSpec as P

HREACH = 2
KB = 9
R = 4
BW = 8
EPSILON = 1e-05
BF = jnp.bfloat16
F32 = jnp.float32
AXES = ("lat", "lon")
VMEM_BYTES = 56 * 1024 * 1024


def shape_of(shape, dtype):
    return jax.ShapeDtypeStruct(tuple(shape), dtype)


def whole(count):
    return [pl.BlockSpec(memory_space=pltpu.VMEM) for _ in range(count)]


def scalars(count):
    return [pl.BlockSpec(memory_space=pltpu.SMEM) for _ in range(count)]


def params():
    return pltpu.CompilerParams(vmem_limit_bytes=VMEM_BYTES)


class Plan:
    def __init__(self, lats, lons, latent, filters, mix_weight, up_weight, down_weight):
        self.lats, self.lons = lats, lons
        self.rows2 = lats // 2
        self.zs = lons // 2
        self.cycles, self.members, self.cells, self.width = latent.shape
        self.basis, _, self.slots, self.band = filters.shape
        self.depth, self.out = mix_weight.shape[1], mix_weight.shape[2]
        self.lift = up_weight.shape[1]
        self.down_rows = down_weight.shape[0]
        self.lanes = self.members * self.depth
        self.meta = self.basis * self.slots * self.band + 2 * self.slots
        self.tail = 16
        self.piece = self.cycles * self.cells + self.tail
        self.kpad = -(-self.depth // 128) * 128
        self.group = 3
        self.parts = self.basis // 3
        self.mix_rows = self.parts * self.depth
        self.rest = self.down_rows - self.depth
        self.rest_rows = -(-self.rest // (3 * 16)) * 16
        self.mlp_rows = self.depth + self.rest_rows
        self.pack_rows = self.mix_rows + self.mlp_rows
        self.pack_lanes = self.group * self.out
        self.total = self.cycles * lats
        self.window = 4 * self.cells

    def fits(self):
        return (
            self.lats % 2 == 0
            and self.lons % 2 == 0
            and self.cells == 8
            and self.members == 2
            and self.slots * self.window == 128
            and self.band // 2 + 2 <= self.cells
            and self.basis % 3 == 0
            and self.lift == 2 * self.out
            and self.depth % 16 == 0
            and self.meta <= self.lanes
            and self.cycles <= self.tail
            and (self.cycles * self.cells) % 16 == 0
            and self.rest > 0
        )


def prep_kernel(plan, spot, latent, gain, meta, mix, up, down, msgs, pack, stage):
    p = plan
    a = spot[0]
    flat = latent[...].astype(F32).reshape(p.cycles * p.members * p.cells, p.width)
    mean = jnp.mean(flat, axis=-1, keepdims=True)
    centered = flat - mean
    variance = jnp.mean(centered * centered, axis=-1, keepdims=True)
    normal = centered * lax.rsqrt(variance + EPSILON) * gain[...]
    normal = normal.reshape(p.cycles, p.members, p.cells, p.width)
    body = p.cycles * p.cells
    for e in range(p.members):
        part = normal[:, e].reshape(body, p.width).astype(BF)
        for q in range(p.lats):
            slot = lax.rem(q - a + p.lats, p.lats)
            stage[slot, 0:body, e * p.depth : (e + 1) * p.depth] = part[
                :, q * p.depth : (q + 1) * p.depth
            ]
    for s in range(p.lats):
        msgs[s][0:body, :] = stage[s, 0:body, :]
        msgs[s][body:, :] = meta[...]
    for k in range(p.basis):
        u, v = k // p.group, k % p.group
        pack[u * p.depth : (u + 1) * p.depth, v * p.out : (v + 1) * p.out] = mix[k]
    base = p.mix_rows
    pack[base : base + p.depth, 0 : p.lift] = up[...]
    pack[base : base + p.depth, p.lift : p.lift + p.out] = down[0 : p.depth, :]
    base += p.depth
    for g in range(3):
        lo = p.depth + g * p.rest_rows
        hi = min(lo + p.rest_rows, p.down_rows)
        if hi > lo:
            pack[base : base + hi - lo, g * p.out : (g + 1) * p.out] = down[lo:hi, :]
        if hi - lo < p.rest_rows:
            gap = p.rest_rows - max(hi - lo, 0)
            pack[base + p.rest_rows - gap : base + p.rest_rows, g * p.out : (g + 1) * p.out] = (
                jnp.zeros((gap, p.out), BF)
            )


def prepare(plan, spot, latent, gain, meta, mix, up, down):
    p = plan
    outs = pl.pallas_call(
        lambda *refs: prep_kernel(
            p, *refs[:7], refs[7 : 7 + p.lats], refs[7 + p.lats], refs[8 + p.lats]
        ),
        out_shape=[shape_of((p.piece, p.lanes), BF)] * p.lats
        + [shape_of((p.pack_rows, p.pack_lanes), BF)],
        in_specs=scalars(1) + whole(6),
        out_specs=whole(p.lats + 1),
        scratch_shapes=[pltpu.VMEM((p.lats, p.cycles * p.cells, p.lanes), BF)],
        compiler_params=params(),
        name="normalize_pack",
    )(spot, latent, gain, meta, mix, up, down)
    return outs[: p.lats], outs[p.lats]


def conv_kernel(plan, spot, rows, taps, own, pair, near, far, packs, keep, send, scratch):
    p = plan
    grid, contracted, slots, mixing = scratch
    a, z, x = spot[0], spot[1], spot[2]
    even = x == 0
    body = p.cycles * p.cells
    grid[...] = jnp.zeros_like(grid)
    for s in range(p.lats):
        band = lax.rem(a - s + p.lats, p.lats)
        lo = s * p.piece

        def read(ref):
            return ref[lo : lo + body, :].astype(F32)

        mine, other, first, second = read(own), read(pair), read(near), read(far)
        blocks = (
            jnp.where(even, first, second),
            jnp.where(even, mine, other),
            jnp.where(even, other, mine),
            jnp.where(even, second, first),
        )
        joined = jnp.concatenate(
            [block.reshape(p.cycles, p.cells, p.lanes) for block in blocks], axis=1
        ).astype(BF)
        where = HREACH + band * p.cycles
        for e in range(p.members):
            grid[pl.ds(where, p.cycles), :, e * p.kpad : e * p.kpad + p.depth] = joined[
                :, :, e * p.depth : (e + 1) * p.depth
            ]

    mixing[...] = jnp.zeros_like(mixing)
    for s in range(p.zs):
        slots[lax.rem(z - s + p.zs, p.zs)] = packs[s][0 : p.mix_rows, :]
    for b in range(p.zs):
        for k in range(p.basis):
            u, v = k // p.group, k % p.group
            mixing[k * p.kpad : k * p.kpad + p.depth, b * p.out : (b + 1) * p.out] = slots[
                b, u * p.depth : (u + 1) * p.depth, v * p.out : (v + 1) * p.out
            ]

    double = 2 * p.cells

    def contract(i, carry):
        source = jnp.concatenate(
            [grid[i + HREACH + rows[i * p.slots + r]] for r in range(p.slots)], axis=0
        )
        tap = taps[i]
        lhs = jnp.concatenate(
            [
                pltpu.roll(
                    jnp.broadcast_to(tap[k : k + 1, :], (double, 128)),
                    0,
                    1,
                    stride=1,
                    stride_axis=0,
                )
                for k in range(p.basis)
            ],
            axis=0,
        ).astype(BF)
        result = jnp.dot(lhs, source, preferred_element_type=F32).astype(BF)
        at = i * (p.members * double)
        for e in range(p.members):
            for k in range(p.basis):
                contracted[
                    pl.ds(pl.multiple_of(at + e * double, double), double),
                    k * p.kpad : (k + 1) * p.kpad,
                ] = result[k * double : (k + 1) * double, e * p.kpad : (e + 1) * p.kpad]
        return carry

    lax.fori_loop(0, p.total, contract, 0, unroll=4)

    count = p.cycles * p.members * double
    core = lax.rem(a, 2)
    for t in range(p.rows2):
        y = lax.rem(a // 2 + t, p.rows2)
        for mate in range(2):
            band = 2 * y + (core if mate == 0 else 1 - core)
            at = pl.multiple_of(band * count, count)
            total = jnp.dot(
                contracted[pl.ds(at, count), :], mixing[...], preferred_element_type=F32
            ).reshape(p.cycles * p.members, 2, p.cells, p.zs * p.out)
            half = count // 2
            left = total[:, 0].reshape(half, p.zs * p.out)
            right = total[:, 1].reshape(half, p.zs * p.out)
            for w in range(2):
                value = jnp.where((x ^ w) == 0, left, right)
                if mate == 0:
                    keep[2 * t + w] = value
                else:
                    send[2 * t + w] = value.astype(BF)


def convolve(plan, spot, rows, taps, own, pair, near, far, packs):
    p = plan
    half = p.cycles * p.members * p.cells
    out = p.zs * p.out

    def body(*refs):
        fixed, rest = refs[:7], refs[7:]
        conv_kernel(p, *fixed, rest[: p.zs], rest[p.zs], rest[p.zs + 1], rest[p.zs + 2 :])

    return pl.pallas_call(
        body,
        out_shape=[
            shape_of((2 * p.rows2, half, out), F32),
            shape_of((2 * p.rows2, half, out), BF),
        ],
        in_specs=scalars(2) + whole(5 + p.zs),
        out_specs=whole(2),
        scratch_shapes=[
            pltpu.VMEM((p.total + 2 * HREACH, p.window, p.members * p.kpad), BF),
            pltpu.VMEM((p.total * p.members * 2 * p.cells, p.basis * p.kpad), BF),
            pltpu.VMEM((p.zs, p.mix_rows, p.pack_lanes), BF),
            pltpu.VMEM((p.basis * p.kpad, out), BF),
        ],
        compiler_params=params(),
        name="contract_mix",
    )(spot, rows, taps, own, pair, near, far, *packs)


def add_kernel(keep, arrived, own, *msgs):
    for i in range(keep.shape[0]):
        value = keep[i] + arrived[i].astype(F32)
        if i == 0:
            own[...] = value
        else:
            msgs[i - 1][...] = value.astype(BF)


def add_cores(keep, arrived):
    count, half, out = keep.shape
    outs = pl.pallas_call(
        add_kernel,
        out_shape=[shape_of((half, out), F32)] + [shape_of((half, out), BF)] * (count - 1),
        in_specs=whole(2),
        out_specs=whole(count),
        compiler_params=params(),
        name="add_cores",
    )(keep, arrived)
    return outs[0], outs[1:]


def unpack_kernel(plan, spot, stacks, up, down, slots):
    p = plan
    a, z, x = spot[0], spot[1], spot[2]
    core = lax.rem(a, 2)
    for mate in range(2):
        for t in range(p.rows2):
            y = lax.rem(a // 2 - t + p.rows2, p.rows2)
            lat = 2 * y + (core if mate == 0 else 1 - core)
            for w in range(2):
                for s in range(p.zs):
                    lon = 2 * lax.rem(z - s + p.zs, p.zs) + (x ^ w)
                    index = (t * 2 + w) * p.zs + s
                    slots[lat * p.lons + lon] = stacks[mate][
                        index * p.mlp_rows : (index + 1) * p.mlp_rows, :
                    ]
    for a in range(p.lats):
        for b in range(p.lons):
            i = a * p.lons + b
            up[a * p.depth : (a + 1) * p.depth, b * p.lift : (b + 1) * p.lift] = slots[
                i, 0 : p.depth, 0 : p.lift
            ]
            base = a * p.down_rows
            cols = slice(b * p.out, (b + 1) * p.out)
            down[base : base + p.depth, cols] = slots[
                i, 0 : p.depth, p.lift : p.lift + p.out
            ]
            for g in range(3):
                lo = p.depth + g * p.rest_rows
                hi = min(lo + p.rest_rows, p.down_rows)
                if hi > lo:
                    down[base + lo : base + hi, cols] = slots[
                        i, p.depth : p.depth + hi - lo, g * p.out : (g + 1) * p.out
                    ]


def unpack(plan, spot, mine, sibling):
    p = plan
    return pl.pallas_call(
        lambda spot, one, two, up, down, slots: unpack_kernel(
            p, spot, (one, two), up, down, slots
        ),
        out_shape=[
            shape_of((p.lats * p.depth, p.lons * p.lift), BF),
            shape_of((p.lats * p.down_rows, p.lons * p.out), BF),
        ],
        in_specs=scalars(1) + whole(2),
        out_specs=whole(2),
        scratch_shapes=[pltpu.VMEM((p.lats * p.lons, p.mlp_rows, p.pack_lanes), BF)],
        compiler_params=params(),
        name="mlp_weights",
    )(spot, mine, sibling)


def mlp_kernel(plan, spot, latent, bias, up, down, own, *rest):
    p = plan
    arrived, (out, conv) = rest[:-2], rest[-2:]
    even = spot[2] == 0
    mine = own[...]
    other = None
    for i, ref in enumerate(arrived):
        value = ref[...].astype(F32)
        if (i + 1) % 2 == 0:
            mine = mine + value
        else:
            other = value if other is None else other + value
    first = jnp.where(even, mine, other)
    second = jnp.where(even, other, mine)
    for b in range(p.zs):
        cols = slice(b * p.out, (b + 1) * p.out)
        conv[:, 2 * b * p.out : (2 * b + 1) * p.out] = first[:, cols]
        conv[:, (2 * b + 1) * p.out : (2 * b + 2) * p.out] = second[:, cols]
    half = p.cycles * p.members * p.cells
    hidden = (latent[...].astype(F32).reshape(half, p.width) + conv[...]).astype(BF)
    lifted = jnp.dot(hidden, up[...], preferred_element_type=F32) + bias[...]
    activated = (lifted * (1.0 + lax.erf(lifted * (0.5**0.5))) * 0.5).astype(BF)
    result = hidden.astype(F32) + jnp.dot(activated, down[...], preferred_element_type=F32)
    out[...] = result.astype(BF).reshape(out.shape)


def mlp(plan, spot, latent, bias, up, down, own, arrived):
    p = plan
    half = p.cycles * p.members * p.cells
    return pl.pallas_call(
        lambda *refs: mlp_kernel(p, *refs),
        out_shape=shape_of(latent.shape, BF),
        in_specs=scalars(1) + whole(5 + len(arrived)),
        out_specs=pl.BlockSpec(memory_space=pltpu.VMEM),
        scratch_shapes=[pltpu.VMEM((half, p.width), F32)],
        compiler_params=params(),
        name="sum_mlp",
    )(spot, latent, bias, up, down, own, *arrived)


def mover(plan):
    p = plan

    def move(value, target):
        pairs = []
        for a in range(p.lats):
            for b in range(p.lons):
                c, d = target(a, b)
                pairs.append((a * p.lons + b, (c % p.lats) * p.lons + d % p.lons))
        return lax.ppermute(value, AXES, pairs)

    return move


def shards_fast(
    plan,
    latent,
    norm_gain,
    filters,
    row_offsets,
    col_offsets,
    mix_weight,
    up_weight,
    up_bias,
    down_weight,
):
    p = plan
    move = mover(p)
    a, b = lax.axis_index("lat"), lax.axis_index("lon")
    spot = jnp.stack([a, b // 2, b % 2]).astype(jnp.int32)
    meta = jnp.concatenate(
        [
            filters.transpose(1, 0, 2, 3).reshape(p.cycles, -1),
            row_offsets.astype(BF),
            col_offsets.astype(BF),
        ],
        axis=1,
    )
    meta = jnp.pad(meta, ((0, p.tail - p.cycles), (0, p.lanes - p.meta)))
    msgs, pack = prepare(
        p, spot, latent, norm_gain.reshape(1, -1), meta, mix_weight, up_weight, down_weight
    )
    pieces = [msgs[0]]
    for s in range(1, p.lats):
        pieces.append(move(msgs[s], lambda i, j, s=s: (i + s, j)))
    packs = [pack]
    for s in range(1, p.zs):
        packs.append(move(pack, lambda i, j, s=s: (i, j + 2 * s)))
    own = jnp.concatenate(pieces, axis=0)
    pair = move(own, lambda i, j: (i, j ^ 1))
    near = move(own, lambda i, j: (i, j + 1 if j % 2 else j - 1))
    far = move(own, lambda i, j: (i, j + 2 if j % 2 else j - 2))

    infos = own.reshape(p.lats, p.piece, p.lanes)[:, p.piece - p.tail :][:, : p.cycles, : p.meta]
    order = (a - jnp.arange(p.lats, dtype=jnp.int32)) % p.lats
    infos = infos[order].reshape(p.total, p.meta)
    split = p.basis * p.slots * p.band
    offsets = infos[:, split:].astype(jnp.int32)
    rows = offsets[:, : p.slots].reshape(-1)
    starts = offsets[:, p.slots :] + p.cells
    values = infos[:, :split].astype(F32).reshape(p.total, p.basis, p.slots, 1, p.band)
    place = (
        jnp.arange(p.window, dtype=jnp.int32)[:, None]
        - jnp.arange(p.band, dtype=jnp.int32)[None, :]
    )
    hits = place[None, None] == starts[:, :, None, None]
    taps = jnp.sum(jnp.where(hits[:, None], values, 0.0), axis=-1)
    taps = taps.reshape(p.total, p.basis, p.slots * p.window)
    taps = jnp.pad(taps, ((0, 0), (0, 16 - p.basis), (0, 0)))

    share = jnp.concatenate([piece[p.mix_rows :] for piece in packs], axis=0)
    share = jnp.concatenate([share, move(share, lambda i, j: (i, j ^ 1))], axis=0)
    bands = [share]
    for t in range(1, p.rows2):
        bands.append(move(share, lambda i, j, t=t: (i + 2 * t, j)))
    share = jnp.concatenate(bands, axis=0)
    sibling = move(share, lambda i, j: (i ^ 1, j))
    up, down = unpack(p, spot, share, sibling)

    keep, send = convolve(p, spot, rows, taps, own, pair, near, far, packs)
    arrived = move(send, lambda i, j: (i ^ 1, j))
    mine, outgoing = add_cores(keep, arrived)
    incoming = []
    for index, value in enumerate(outgoing):
        t, w = (index + 1) // 2, (index + 1) % 2
        incoming.append(move(value, lambda i, j, t=t, w=w: (i + 2 * t, j ^ w)))
    return mlp(p, spot, latent, up_bias.reshape(1, -1), up, down, mine, incoming)


def padded(shard, sides, width, wrap):
    for axis, dim in sides:
        size, length = (lax.axis_size(axis), shard.shape[dim])
        up = [(i, (i + 1) % size) for i in range(size if wrap else size - 1)]
        down = [(j, i) for i, j in up]
        last = lax.slice_in_dim(shard, length - width, length, axis=dim)
        leading = lax.slice_in_dim(shard, 0, width, axis=dim)
        before = lax.ppermute(last, axis, up)
        after = lax.ppermute(leading, axis, down)
        shard = jnp.concatenate([before, shard, after], axis=dim)
    return shard


def normalize(latent, norm_gain):
    widened = latent.astype(jnp.float32)
    channel_mean = jnp.mean(widened, axis=-1, keepdims=True)
    centered = widened - channel_mean
    variance = jnp.mean(centered * centered, axis=-1, keepdims=True)
    return (centered * lax.rsqrt(variance + EPSILON) * norm_gain).astype(jnp.bfloat16)


def contract_cycles(
    band_slab, filters, row_offsets, col_offsets, cycle_count, out_cells, shift_cells
):
    members = band_slab.shape[1]
    channel_share = band_slab.shape[3]

    def cycle_output(cycle_index):
        pieces = []
        for row_slot in range(R):
            where = cycle_index + HREACH + row_offsets[cycle_index, row_slot]
            source = lax.dynamic_index_in_dim(band_slab, where, 0, keepdims=False)
            start = col_offsets[cycle_index, row_slot] + shift_cells
            segment = lax.dynamic_slice_in_dim(source, start, out_cells + BW - 1, 1)
            for band_step in range(BW):
                pieces.append(segment[:, band_step : band_step + out_cells])
        stacked = jnp.stack(pieces).reshape(R * BW, members * out_cells * channel_share)
        cycle_filter = lax.dynamic_index_in_dim(filters, cycle_index, 1, keepdims=False).reshape(
            KB, R * BW
        )
        contracted = jnp.dot(cycle_filter, stacked, preferred_element_type=jnp.float32).astype(
            jnp.bfloat16
        )
        return contracted.reshape(KB, members, out_cells, channel_share)

    return lax.map(cycle_output, jnp.arange(cycle_count, dtype=jnp.int32))


def shards_plain(
    latent,
    norm_gain,
    filters,
    row_offsets,
    col_offsets,
    mix_weight,
    up_weight,
    up_bias,
    down_weight,
):
    cycle_count = latent.shape[0]
    local_cells = latent.shape[2]
    width = latent.shape[3]
    partial_weights = (
        lax.all_gather(mix_weight, "lat", axis=1, tiled=True),
        lax.all_gather(up_weight, "lat", axis=0, tiled=True),
        lax.all_gather(down_weight, "lat", axis=0, tiled=True),
    )
    mix_full, up_full, down_full = (
        lax.all_gather(partial_weights[0], "lon", axis=2, tiled=True),
        lax.all_gather(partial_weights[1], "lon", axis=1, tiled=True),
        lax.all_gather(partial_weights[2], "lon", axis=1, tiled=True),
    )
    normalized = normalize(latent, norm_gain)
    side_reach = BW // 2 + 2
    cycle_rims = padded(normalized, (("lat", 0),), HREACH, False)
    band_slab = padded(cycle_rims, (("lon", 2),), side_reach, True)
    contracted = contract_cycles(
        band_slab, filters, row_offsets, col_offsets, cycle_count, local_cells, side_reach
    )
    convolved = jnp.einsum(
        "ikejc,kcd->iejd", contracted, mix_full, preferred_element_type=jnp.float32
    )
    hidden = (latent.astype(jnp.float32) + convolved).astype(jnp.bfloat16)
    flattened = hidden.reshape(-1, width)
    lifted = jnp.dot(flattened, up_full, preferred_element_type=jnp.float32) + up_bias
    activated = jax.nn.gelu(lifted, approximate=False).astype(jnp.bfloat16)
    result = flattened.astype(jnp.float32) + jnp.dot(
        activated, down_full, preferred_element_type=jnp.float32
    )
    return result.astype(jnp.bfloat16).reshape(latent.shape)


def solution(mesh):
    lats, lons = mesh.shape["lat"], mesh.shape["lon"]

    def shards(*args):
        latent, _, filters, _, _, mix_weight, up_weight, _, down_weight = args
        plan = Plan(lats, lons, latent, filters, mix_weight, up_weight, down_weight)
        if plan.fits():
            return shards_fast(plan, *args)
        return shards_plain(*args)

    in_specs = (
        P("lat", None, "lon", None),
        P(),
        P(None, "lat", None, None),
        P("lat", None),
        P("lat", None),
        P(None, "lat", "lon"),
        P("lat", "lon"),
        P(),
        P("lat", "lon"),
    )
    out_specs = P("lat", None, "lon", None)
    return jax.shard_map(shards, mesh=mesh, in_specs=in_specs, out_specs=out_specs, check_vma=False)
```

```python
import jax
import jax.numpy as jnp
from jax import lax
from jax.experimental import pallas as pl
from jax.experimental.pallas import tpu as pltpu
from jax.sharding import PartitionSpec as P

HREACH = 2
KB = 9
R = 4
BW = 8
EPSILON = 1e-05
BF = jnp.bfloat16
F32 = jnp.float32
AXES = ("lat", "lon")


def shape_of(shape, dtype):
    return jax.ShapeDtypeStruct(tuple(shape), dtype)


def whole(count):
    return [pl.BlockSpec(memory_space=pltpu.VMEM) for _ in range(count)]


def scalars(count):
    return [pl.BlockSpec(memory_space=pltpu.SMEM) for _ in range(count)]


def params(mebibytes=24):
    return pltpu.CompilerParams(vmem_limit_bytes=mebibytes * 1024 * 1024)


class Plan:
    def __init__(self, lats, lons, latent, filters, mix_weight, up_weight, down_weight):
        self.lats, self.lons = lats, lons
        self.ys = lats // 2
        self.zs = lons // 2
        self.cycles, self.members, self.cells, self.width = latent.shape
        self.basis, _, self.slots, self.band = filters.shape
        self.depth, self.out = mix_weight.shape[1], mix_weight.shape[2]
        self.lift = up_weight.shape[1]
        self.down_rows = down_weight.shape[0]
        self.half = self.cycles * self.members * self.cells
        self.body = self.cycles * self.cells
        self.lanes = self.members * self.depth
        self.wide = -(-self.lanes // 128) * 128
        self.taps_row = self.wide // 128
        self.groups = -(-self.cycles // self.taps_row)
        self.piece = self.body + 16 * self.groups
        self.kpad = -(-self.depth // 128) * 128
        self.group = 3
        self.mix_rows = (self.basis // 3) * self.depth
        self.mix_lanes = -(-self.group * self.out // 128) * 128
        self.mlp_lanes = 8 * self.out
        self.total = self.cycles * lats
        self.window = 4 * self.cells
        self.double = 2 * self.cells

    def fits(self):
        return (
            self.lats == 4
            and self.lons % 2 == 0
            and self.cells == 8
            and self.members == 2
            and self.slots * self.window == 128
            and self.band == 8
            and self.basis % 3 == 0
            and self.basis < 16
            and self.lift == 2 * self.out
            and self.depth == self.lift
            and self.down_rows == 4 * self.out
            and self.out % 16 == 0
            and self.mlp_lanes % 128 == 0
            and self.body % 16 == 0
        )


def place():
    a, b = lax.axis_index("lat"), lax.axis_index("lon")
    return a, b // 2, b % 2


def normal_kernel(plan, rows, cols, latent, gain, filters, *rest):
    p = plan
    msgs, stage = rest[: p.lats], rest[p.lats]
    a, _, _ = place()
    flat = latent[...].astype(F32).reshape(p.half, p.width)
    mean = jnp.mean(flat, axis=-1, keepdims=True)
    centered = flat - mean
    variance = jnp.mean(centered * centered, axis=-1, keepdims=True)
    normal = centered * lax.rsqrt(variance + EPSILON) * gain[...]
    normal = normal.reshape(p.cycles, p.members, p.cells, p.width)
    for e in range(p.members):
        part = normal[:, e].reshape(p.body, p.width).astype(BF)
        for q in range(p.lats):
            slot = lax.rem(q - a + p.lats, p.lats)
            stage[slot, :, e * p.depth : (e + 1) * p.depth] = part[
                :, q * p.depth : (q + 1) * p.depth
            ]
    row = lax.broadcasted_iota(jnp.int32, (p.slots * p.band, 128), 0)
    lane = lax.broadcasted_iota(jnp.int32, (p.slots * p.band, 128), 1)
    first = lax.broadcasted_iota(jnp.int32, (16, 128), 0)
    second = lax.broadcasted_iota(jnp.int32, (16, 128), 1)
    tails = []
    for g in range(p.groups):
        blocks = []
        for i in range(g * p.taps_row, (g + 1) * p.taps_row):
            if i >= p.cycles:
                blocks.append(jnp.zeros((16, 128), F32))
                continue
            target = jnp.zeros((p.slots * p.band, 128), jnp.int32)
            offset = jnp.zeros((16, 128), jnp.int32)
            for r in range(p.slots):
                start = r * p.window + p.cells + cols[r, i] - r * p.band
                target = jnp.where(row // p.band == r, start + row, target)
                offset = jnp.where(second == r, rows[r, i], offset)
            hit = jnp.where(lane == target, 1.0, 0.0).astype(BF)
            taps = lax.dot_general(
                filters[i], hit, (((0,), (0,)), ((), ())), preferred_element_type=F32
            )
            taps = jnp.concatenate([taps, jnp.zeros((16 - p.basis, 128), F32)], axis=0)
            blocks.append(jnp.where(first == p.basis, offset.astype(F32), taps))
        tails.append(jnp.concatenate(blocks, axis=1).astype(BF))
    for s in range(p.lats):
        msgs[s][0 : p.body, 0 : p.lanes] = stage[s]
        if p.wide > p.lanes:
            msgs[s][0 : p.body, p.lanes :] = jnp.zeros((p.body, p.wide - p.lanes), BF)
        for g in range(p.groups):
            msgs[s][p.body + 16 * g : p.body + 16 * (g + 1), :] = tails[g]


def normal_pieces(plan, rows, cols, latent, gain, filters):
    p = plan
    return pl.pallas_call(
        lambda *refs: normal_kernel(p, *refs),
        out_shape=[shape_of((p.piece, p.wide), BF)] * p.lats,
        in_specs=scalars(2) + whole(3),
        out_specs=whole(p.lats),
        scratch_shapes=[pltpu.VMEM((p.lats, p.body, p.lanes), BF)],
        compiler_params=params(60),
        name="normalize",
    )(rows, cols, latent, gain, filters)


def pack_kernel(plan, mix, up, down, mlp_pack, mix_pack):
    p = plan
    for q in range(p.lift // p.out):
        mlp_pack[:, q * p.depth : (q + 1) * p.depth] = up[q * p.out : (q + 1) * p.out, :]
    mlp_pack[:, 2 * p.depth :] = down[...]
    for k in range(p.basis):
        u, v = k // p.group, k % p.group
        mix_pack[u * p.depth : (u + 1) * p.depth, v * p.out : (v + 1) * p.out] = mix[k]
    used = p.group * p.out
    if p.mix_lanes > used:
        mix_pack[:, used:] = jnp.zeros((p.mix_rows, p.mix_lanes - used), BF)


def pack_weights(plan, mix, up, down):
    p = plan
    return pl.pallas_call(
        lambda *refs: pack_kernel(p, *refs),
        out_shape=[
            shape_of((p.out, p.mlp_lanes), BF),
            shape_of((p.mix_rows, p.mix_lanes), BF),
        ],
        in_specs=whole(3),
        out_specs=whole(2),
        compiler_params=params(60),
        name="pack_weights",
    )(mix, up, down)


def contract_kernel(plan, own, pair, near, far, *rest):
    p = plan
    pieces = rest[: p.lats]
    contracted, grid, taps, numbers, table, done = rest[p.lats :]
    a, z, x = place()
    even = x == 0
    for s in range(p.lats):
        for g in range(p.groups):
            lo = p.body + 16 * g
            block = pieces[s][lo : lo + 16, :].astype(F32)
            for i in range(p.taps_row):
                if g * p.taps_row + i < p.cycles:
                    taps[s * p.cycles + g * p.taps_row + i] = block[:, i * 128 : (i + 1) * 128]
            numbers[8 * (s * p.groups + g) : 8 * (s * p.groups + g) + 8, :] = block[
                8:16, :
            ].astype(jnp.int32)
    load = pltpu.make_async_copy(numbers, table, done)
    load.start()
    edge = jnp.zeros((HREACH,) + grid.shape[1:], BF)
    grid[0:HREACH] = edge
    grid[HREACH + p.total : 2 * HREACH + p.total] = edge
    gap = p.kpad - p.depth
    for s in range(p.lats):
        band = lax.rem(a - s + p.lats, p.lats)
        lo = s * p.body

        def read(ref):
            return ref[lo : lo + p.body, 0 : p.lanes].astype(F32)

        mine, other, first, second = read(own), read(pair), read(near), read(far)
        blocks = (
            jnp.where(even, first, second),
            jnp.where(even, mine, other),
            jnp.where(even, other, mine),
            jnp.where(even, second, first),
        )
        joined = jnp.concatenate(
            [block.reshape(p.cycles, p.cells, p.lanes) for block in blocks], axis=1
        ).astype(BF)
        where = HREACH + band * p.cycles
        for e in range(p.members):
            grid[pl.ds(where, p.cycles), :, e * p.kpad : e * p.kpad + p.depth] = joined[
                :, :, e * p.depth : (e + 1) * p.depth
            ]
            if gap:
                grid[pl.ds(where, p.cycles), :, e * p.kpad + p.depth : (e + 1) * p.kpad] = (
                    jnp.zeros((p.cycles, p.window, gap), BF)
                )
    load.wait()

    for s in range(p.lats):
        band = lax.rem(a - s + p.lats, p.lats)
        for c in range(p.cycles):
            i = band * p.cycles + c
            line = 8 * (s * p.groups + c // p.taps_row) + p.basis - 8
            lane = (c % p.taps_row) * 128
            source = jnp.concatenate(
                [grid[i + HREACH + table[line, lane + r]] for r in range(p.slots)], axis=0
            )
            lhs = jnp.concatenate(
                [
                    pltpu.roll(
                        jnp.broadcast_to(
                            taps[s * p.cycles + c, k : k + 1, :], (p.double, 128)
                        ),
                        0,
                        1,
                        stride=1,
                        stride_axis=0,
                    )
                    for k in range(p.basis)
                ],
                axis=0,
            ).astype(BF)
            result = jnp.dot(lhs, source, preferred_element_type=F32).astype(BF)
            at = i * (p.members * p.double)
            for e in range(p.members):
                for k in range(p.basis):
                    contracted[
                        pl.ds(pl.multiple_of(at + e * p.double, p.double), p.double),
                        k * p.kpad : (k + 1) * p.kpad,
                    ] = result[
                        k * p.double : (k + 1) * p.double, e * p.kpad : (e + 1) * p.kpad
                    ]


def contract(plan, own, pair, near, far, pieces):
    p = plan
    lines = 8 * p.lats * p.groups
    return pl.pallas_call(
        lambda *refs: contract_kernel(p, *refs),
        out_shape=shape_of((p.total * p.members * p.double, p.basis * p.kpad), BF),
        in_specs=whole(4 + p.lats),
        out_specs=pl.BlockSpec(memory_space=pltpu.VMEM),
        scratch_shapes=[
            pltpu.VMEM((p.total + 2 * HREACH, p.window, p.members * p.kpad), BF),
            pltpu.VMEM((p.total, 16, 128), F32),
            pltpu.VMEM((lines, p.wide), jnp.int32),
            pltpu.SMEM((lines, p.wide), jnp.int32),
            pltpu.SemaphoreType.DMA,
        ],
        compiler_params=params(),
        name="contract",
    )(own, pair, near, far, *pieces)


def mix_kernel(plan, contracted, *rest):
    p = plan
    packs = rest[: p.zs]
    keep, send, slots, mixing = rest[p.zs :]
    a, z, x = place()
    if p.kpad > p.depth:
        for k in range(p.basis):
            mixing[k * p.kpad + p.depth : (k + 1) * p.kpad, :] = jnp.zeros(
                (p.kpad - p.depth, p.zs * p.out), BF
            )
    for s in range(p.zs):
        slots[lax.rem(z - s + p.zs, p.zs)] = packs[s][...]
    for b in range(p.zs):
        for k in range(p.basis):
            u, v = k // p.group, k % p.group
            mixing[k * p.kpad : k * p.kpad + p.depth, b * p.out : (b + 1) * p.out] = slots[
                b, u * p.depth : (u + 1) * p.depth, v * p.out : (v + 1) * p.out
            ]
    count = 2 * p.half
    core = lax.rem(a, 2)
    for t in range(p.ys):
        y = lax.rem(a // 2 + t, p.ys)
        for mate in range(2):
            band = 2 * y + (core if mate == 0 else 1 - core)
            at = pl.multiple_of(band * count, count)
            total = jnp.dot(
                contracted[pl.ds(at, count), :], mixing[...], preferred_element_type=F32
            ).reshape(p.cycles * p.members, 2, p.cells, p.zs * p.out)
            left = total[:, 0].reshape(p.half, p.zs * p.out)
            right = total[:, 1].reshape(p.half, p.zs * p.out)
            for w in range(2):
                value = jnp.where((x ^ w) == 0, left, right)
                if mate == 0:
                    keep[2 * t + w] = value
                else:
                    send[2 * t + w] = value.astype(BF)


def mix_basis(plan, contracted, packs):
    p = plan
    out = p.zs * p.out
    return pl.pallas_call(
        lambda *refs: mix_kernel(p, *refs),
        out_shape=[
            shape_of((2 * p.ys, p.half, out), F32),
            shape_of((2 * p.ys, p.half, out), BF),
        ],
        in_specs=whole(1 + p.zs),
        out_specs=whole(2),
        scratch_shapes=[
            pltpu.VMEM((p.zs, p.mix_rows, p.mix_lanes), BF),
            pltpu.VMEM((p.basis * p.kpad, out), BF),
        ],
        compiler_params=params(),
        name="mix_basis",
    )(contracted, *packs)


def add_kernel(keep, arrived, own, *msgs):
    for i in range(keep.shape[0]):
        value = keep[i] + arrived[i].astype(F32)
        if i == 0:
            own[...] = value
        else:
            msgs[i - 1][...] = value.astype(BF)


def add_cores(keep, arrived):
    count, half, out = keep.shape
    outs = pl.pallas_call(
        add_kernel,
        out_shape=[shape_of((half, out), F32)] + [shape_of((half, out), BF)] * (count - 1),
        in_specs=whole(2),
        out_specs=whole(count),
        compiler_params=params(),
        name="add_cores",
    )(keep, arrived)
    return outs[0], outs[1:]


def unpack_kernel(plan, mine, sibling, up, down, slots):
    p = plan
    a, z, x = place()
    core = lax.rem(a, 2)
    for mate, stack in enumerate((mine, sibling)):
        c = core if mate == 0 else 1 - core
        for step in range(4):
            low, high = step % 2, step // 2
            dx = jnp.where(c == 0, low, high)
            dy = jnp.where(c == 0, high, low)
            lat = 2 * ((a // 2) ^ dy) + c
            for s in range(p.zs):
                lon = 2 * lax.rem(z - s + p.zs, p.zs) + (x ^ dx)
                index = step * p.zs + s
                slots[lat * p.lons + lon] = stack[index * p.out : (index + 1) * p.out, :]
    for a in range(p.lats):
        for b in range(p.lons):
            i = a * p.lons + b
            for q in range(p.lift // p.out):
                up[
                    a * p.depth + q * p.out : a * p.depth + (q + 1) * p.out,
                    b * p.lift : (b + 1) * p.lift,
                ] = slots[i, :, q * p.depth : (q + 1) * p.depth]
            down[
                b * p.out : (b + 1) * p.out, a * p.down_rows : (a + 1) * p.down_rows
            ] = slots[i, :, 2 * p.depth :]


def unpack(plan, mine, sibling):
    p = plan
    return pl.pallas_call(
        lambda *refs: unpack_kernel(p, *refs),
        out_shape=[
            shape_of((p.lats * p.depth, p.lons * p.lift), BF),
            shape_of((p.lons * p.out, p.lats * p.down_rows), BF),
        ],
        in_specs=whole(2),
        out_specs=whole(2),
        scratch_shapes=[pltpu.VMEM((p.lats * p.lons, p.out, p.mlp_lanes), BF)],
        compiler_params=params(),
        name="mlp_weights",
    )(mine, sibling)


def mlp_kernel(plan, latent, bias, up, down, own, *rest):
    p = plan
    arrived, (out, conv) = rest[:-2], rest[-2:]
    _, _, x = place()
    even = x == 0
    mine = own[...]
    other = None
    for i, ref in enumerate(arrived):
        value = ref[...].astype(F32)
        if (i + 1) % 2 == 0:
            mine = mine + value
        else:
            other = value if other is None else other + value
    first = jnp.where(even, mine, other)
    second = jnp.where(even, other, mine)
    for b in range(p.zs):
        cols = slice(b * p.out, (b + 1) * p.out)
        conv[:, 2 * b * p.out : (2 * b + 1) * p.out] = first[:, cols]
        conv[:, (2 * b + 1) * p.out : (2 * b + 2) * p.out] = second[:, cols]
    hidden = (latent[...].astype(F32).reshape(p.half, p.width) + conv[...]).astype(BF)
    lifted = jnp.dot(hidden, up[...], preferred_element_type=F32) + bias[...]
    activated = (lifted * (1.0 + lax.erf(lifted * (0.5**0.5))) * 0.5).astype(BF)
    lowered = lax.dot_general(
        activated, down[...], (((1,), (1,)), ((), ())), preferred_element_type=F32
    )
    out[...] = (hidden.astype(F32) + lowered).astype(BF).reshape(out.shape)


def mlp(plan, latent, bias, up, down, own, arrived):
    p = plan
    return pl.pallas_call(
        lambda *refs: mlp_kernel(p, *refs),
        out_shape=shape_of(latent.shape, BF),
        in_specs=whole(5 + len(arrived)),
        out_specs=pl.BlockSpec(memory_space=pltpu.VMEM),
        scratch_shapes=[pltpu.VMEM((p.half, p.width), F32)],
        compiler_params=params(),
        name="sum_mlp",
    )(latent, bias, up, down, own, *arrived)


def mover(plan):
    p = plan

    def move(value, target):
        pairs = []
        for a in range(p.lats):
            for b in range(p.lons):
                c, d = target(a, b)
                pairs.append((a * p.lons + b, (c % p.lats) * p.lons + d % p.lons))
        return lax.ppermute(value, AXES, pairs)

    return move


def after(value, *others):
    return lax.optimization_barrier((value,) + others)[0]


def shards_fast(
    plan,
    latent,
    norm_gain,
    filters,
    row_offsets,
    col_offsets,
    mix_weight,
    up_weight,
    up_bias,
    down_weight,
):
    p = plan
    move = mover(p)
    taps = filters.transpose(1, 2, 3, 0).reshape(p.cycles, p.slots * p.band, p.basis)
    msgs = normal_pieces(
        p, row_offsets.T, col_offsets.T, latent, norm_gain, taps
    )
    pieces = [msgs[0]]
    for s in range(1, p.lats):
        pieces.append(move(msgs[s], lambda i, j, s=s: (i + s, j)))
    mlp_pack, mix_pack = pack_weights(
        p, mix_weight, after(up_weight, msgs[0]), down_weight.T
    )
    shares = [mlp_pack]
    for s in range(1, p.zs):
        shares.append(move(mlp_pack, lambda i, j, s=s: (i, j + 2 * s)))
    own = jnp.concatenate([piece[: p.body] for piece in pieces], axis=0)
    pair = move(own, lambda i, j: (i, j ^ 1))
    near = move(own, lambda i, j: (i, j + 1 if j % 2 else j - 1))
    far = move(own, lambda i, j: (i, j + 2 if j % 2 else j - 2))

    mix_pack = after(mix_pack, own)
    packs = [mix_pack]
    for s in range(1, p.zs):
        packs.append(move(mix_pack, lambda i, j, s=s: (i, j + 2 * s)))

    contracted = contract(p, own, pair, near, far, pieces)
    share = after(jnp.concatenate(shares, axis=0), near, far)
    crossed = move(share, lambda i, j: (i + 2, j) if i % 2 else (i, j ^ 1))
    share = after(jnp.concatenate([share, crossed], axis=0), contracted, packs[1])
    crossed = move(share, lambda i, j: (i, j ^ 1) if i % 2 else (i + 2, j))
    keep, send = mix_basis(p, contracted, packs)
    arrived = move(send, lambda i, j: (i ^ 1, j))
    mine, outgoing = add_cores(keep, arrived)
    share = after(jnp.concatenate([share, crossed], axis=0), mine)
    up, down = unpack(p, share, move(share, lambda i, j: (i ^ 1, j)))
    incoming = []
    for index, value in enumerate(outgoing):
        t, w = (index + 1) // 2, (index + 1) % 2
        incoming.append(move(value, lambda i, j, t=t, w=w: (i + 2 * t, j ^ w)))

    return mlp(p, latent, up_bias, up, down, mine, incoming)


def padded(shard, sides, width, wrap):
    for axis, dim in sides:
        size, length = (lax.axis_size(axis), shard.shape[dim])
        up = [(i, (i + 1) % size) for i in range(size if wrap else size - 1)]
        down = [(j, i) for i, j in up]
        last = lax.slice_in_dim(shard, length - width, length, axis=dim)
        leading = lax.slice_in_dim(shard, 0, width, axis=dim)
        before = lax.ppermute(last, axis, up)
        after = lax.ppermute(leading, axis, down)
        shard = jnp.concatenate([before, shard, after], axis=dim)
    return shard


def normalize(latent, norm_gain):
    widened = latent.astype(jnp.float32)
    channel_mean = jnp.mean(widened, axis=-1, keepdims=True)
    centered = widened - channel_mean
    variance = jnp.mean(centered * centered, axis=-1, keepdims=True)
    return (centered * lax.rsqrt(variance + EPSILON) * norm_gain).astype(jnp.bfloat16)


def contract_cycles(
    band_slab, filters, row_offsets, col_offsets, cycle_count, out_cells, shift_cells
):
    members = band_slab.shape[1]
    channel_share = band_slab.shape[3]

    def cycle_output(cycle_index):
        pieces = []
        for row_slot in range(R):
            where = cycle_index + HREACH + row_offsets[cycle_index, row_slot]
            source = lax.dynamic_index_in_dim(band_slab, where, 0, keepdims=False)
            start = col_offsets[cycle_index, row_slot] + shift_cells
            segment = lax.dynamic_slice_in_dim(source, start, out_cells + BW - 1, 1)
            for band_step in range(BW):
                pieces.append(segment[:, band_step : band_step + out_cells])
        stacked = jnp.stack(pieces).reshape(R * BW, members * out_cells * channel_share)
        cycle_filter = lax.dynamic_index_in_dim(filters, cycle_index, 1, keepdims=False).reshape(
            KB, R * BW
        )
        contracted = jnp.dot(cycle_filter, stacked, preferred_element_type=jnp.float32).astype(
            jnp.bfloat16
        )
        return contracted.reshape(KB, members, out_cells, channel_share)

    return lax.map(cycle_output, jnp.arange(cycle_count, dtype=jnp.int32))


def shards_plain(
    latent,
    norm_gain,
    filters,
    row_offsets,
    col_offsets,
    mix_weight,
    up_weight,
    up_bias,
    down_weight,
):
    cycle_count = latent.shape[0]
    local_cells = latent.shape[2]
    width = latent.shape[3]
    partial_weights = (
        lax.all_gather(mix_weight, "lat", axis=1, tiled=True),
        lax.all_gather(up_weight, "lat", axis=0, tiled=True),
        lax.all_gather(down_weight, "lat", axis=0, tiled=True),
    )
    mix_full, up_full, down_full = (
        lax.all_gather(partial_weights[0], "lon", axis=2, tiled=True),
        lax.all_gather(partial_weights[1], "lon", axis=1, tiled=True),
        lax.all_gather(partial_weights[2], "lon", axis=1, tiled=True),
    )
    normalized = normalize(latent, norm_gain)
    side_reach = BW // 2 + 2
    cycle_rims = padded(normalized, (("lat", 0),), HREACH, False)
    band_slab = padded(cycle_rims, (("lon", 2),), side_reach, True)
    contracted = contract_cycles(
        band_slab, filters, row_offsets, col_offsets, cycle_count, local_cells, side_reach
    )
    convolved = jnp.einsum(
        "ikejc,kcd->iejd", contracted, mix_full, preferred_element_type=jnp.float32
    )
    hidden = (latent.astype(jnp.float32) + convolved).astype(jnp.bfloat16)
    flattened = hidden.reshape(-1, width)
    lifted = jnp.dot(flattened, up_full, preferred_element_type=jnp.float32) + up_bias
    activated = jax.nn.gelu(lifted, approximate=False).astype(jnp.bfloat16)
    result = flattened.astype(jnp.float32) + jnp.dot(
        activated, down_full, preferred_element_type=jnp.float32
    )
    return result.astype(jnp.bfloat16).reshape(latent.shape)


def solution(mesh):
    lats, lons = mesh.shape["lat"], mesh.shape["lon"]

    def shards(*args):
        latent, _, filters, _, _, mix_weight, up_weight, _, down_weight = args
        plan = Plan(lats, lons, latent, filters, mix_weight, up_weight, down_weight)
        if plan.fits():
            return shards_fast(plan, *args)
        return shards_plain(*args)

    in_specs = (
        P("lat", None, "lon", None),
        P(),
        P(None, "lat", None, None),
        P("lat", None),
        P("lat", None),
        P(None, "lat", "lon"),
        P("lat", "lon"),
        P(),
        P("lat", "lon"),
    )
    out_specs = P("lat", None, "lon", None)
    return jax.shard_map(shards, mesh=mesh, in_specs=in_specs, out_specs=out_specs, check_vma=False)
```

```python
import jax
import jax.numpy as jnp
from jax import lax
from jax.experimental import pallas as pl
from jax.experimental.pallas import tpu as pltpu
from jax.sharding import PartitionSpec as P

HREACH = 2
KB = 9
R = 4
BW = 8
EPSILON = 1e-05
BF = jnp.bfloat16
F32 = jnp.float32
AXES = ("lat", "lon")


def shape_of(shape, dtype):
    return jax.ShapeDtypeStruct(tuple(shape), dtype)


def whole(count):
    return [pl.BlockSpec(memory_space=pltpu.VMEM) for _ in range(count)]


def scalars(count):
    return [pl.BlockSpec(memory_space=pltpu.SMEM) for _ in range(count)]


def params(mebibytes=24):
    return pltpu.CompilerParams(vmem_limit_bytes=mebibytes * 1024 * 1024)


class Plan:
    def __init__(self, lats, lons, latent, filters, mix_weight, up_weight, down_weight):
        self.lats, self.lons = lats, lons
        self.ys = lats // 2
        self.zs = lons // 2
        self.cycles, self.members, self.cells, self.width = latent.shape
        self.basis, _, self.slots, self.band = filters.shape
        self.depth, self.out = mix_weight.shape[1], mix_weight.shape[2]
        self.lift = up_weight.shape[1]
        self.down_rows = down_weight.shape[0]
        self.half = self.cycles * self.members * self.cells
        self.body = self.cycles * self.cells
        self.lanes = self.members * self.depth
        self.wide = -(-self.lanes // 128) * 128
        self.taps_row = self.wide // 128
        self.groups = -(-self.cycles // self.taps_row)
        self.piece = self.body + 16 * self.groups
        self.kpad = -(-self.depth // 128) * 128
        self.group = 3
        self.mix_rows = (self.basis // 3) * self.depth
        self.mix_lanes = 256
        self.fold = 2 * self.mix_rows // 5
        self.mlp_lanes = 8 * self.out
        self.total = self.cycles * lats
        self.window = 4 * self.cells
        self.double = 2 * self.cells

    def fits(self):
        return (
            self.lats == 4
            and self.zs == 4
            and self.cells == 8
            and self.members == 2
            and self.slots * self.window == 128
            and self.band == 8
            and self.basis % 3 == 0
            and self.basis < 16
            and self.lift == 2 * self.out
            and self.depth == self.lift
            and self.down_rows == 4 * self.out
            and self.out % 16 == 0
            and self.mlp_lanes == 5 * 128
            and 3 * self.out <= self.mix_lanes
            and self.fold % 32 == 0
            and 5 * self.fold == 2 * self.mix_rows
            and self.body % 16 == 0
        )


def folds(plan):
    p = plan
    places = []
    for c in range(2):
        for h in range(2):
            places.append((0, (2 * c + h) * 128, h * p.fold, c * 128, p.fold))
        places.append((c * (p.fold // 2), 512, 2 * p.fold, c * 128, p.fold // 2))
    return places


def place():
    a, b = lax.axis_index("lat"), lax.axis_index("lon")
    return a, b // 2, b % 2


def normal_kernel(plan, rows, cols, latent, gain, filters, *rest):
    p = plan
    msgs, stage = rest[: p.lats], rest[p.lats]
    a, _, _ = place()
    flat = latent[...].astype(F32).reshape(p.half, p.width)
    mean = jnp.mean(flat, axis=-1, keepdims=True)
    centered = flat - mean
    variance = jnp.mean(centered * centered, axis=-1, keepdims=True)
    normal = centered * lax.rsqrt(variance + EPSILON) * gain[...]
    normal = normal.reshape(p.cycles, p.members, p.cells, p.width)
    for e in range(p.members):
        part = normal[:, e].reshape(p.body, p.width).astype(BF)
        for q in range(p.lats):
            slot = lax.rem(q - a + p.lats, p.lats)
            stage[slot, :, e * p.depth : (e + 1) * p.depth] = part[
                :, q * p.depth : (q + 1) * p.depth
            ]
    row = lax.broadcasted_iota(jnp.int32, (p.slots * p.band, 128), 0)
    lane = lax.broadcasted_iota(jnp.int32, (p.slots * p.band, 128), 1)
    first = lax.broadcasted_iota(jnp.int32, (16, 128), 0)
    second = lax.broadcasted_iota(jnp.int32, (16, 128), 1)
    tails = []
    for g in range(p.groups):
        blocks = []
        for i in range(g * p.taps_row, (g + 1) * p.taps_row):
            if i >= p.cycles:
                blocks.append(jnp.zeros((16, 128), F32))
                continue
            target = jnp.zeros((p.slots * p.band, 128), jnp.int32)
            offset = jnp.zeros((16, 128), jnp.int32)
            for r in range(p.slots):
                start = r * p.window + p.cells + cols[r, i] - r * p.band
                target = jnp.where(row // p.band == r, start + row, target)
                offset = jnp.where(second == r, rows[r, i], offset)
            hit = jnp.where(lane == target, 1.0, 0.0).astype(BF)
            taps = lax.dot_general(
                filters[i], hit, (((0,), (0,)), ((), ())), preferred_element_type=F32
            )
            taps = jnp.concatenate([taps, jnp.zeros((16 - p.basis, 128), F32)], axis=0)
            blocks.append(jnp.where(first == p.basis, offset.astype(F32), taps))
        tails.append(jnp.concatenate(blocks, axis=1).astype(BF))
    for s in range(p.lats):
        msgs[s][0 : p.body, 0 : p.lanes] = stage[s]
        if p.wide > p.lanes:
            msgs[s][0 : p.body, p.lanes :] = jnp.zeros((p.body, p.wide - p.lanes), BF)
        for g in range(p.groups):
            msgs[s][p.body + 16 * g : p.body + 16 * (g + 1), :] = tails[g]


def normal_pieces(plan, rows, cols, latent, gain, filters):
    p = plan
    return pl.pallas_call(
        lambda *refs: normal_kernel(p, *refs),
        out_shape=[shape_of((p.piece, p.wide), BF)] * p.lats,
        in_specs=scalars(2) + whole(3),
        out_specs=whole(p.lats),
        scratch_shapes=[pltpu.VMEM((p.lats, p.body, p.lanes), BF)],
        compiler_params=params(60),
        name="normalize",
    )(rows, cols, latent, gain, filters)


def pack_kernel(plan, mix, up, down, mlp_pack, mix_pack, block):
    p = plan
    for q in range(p.lift // p.out):
        mlp_pack[:, q * p.depth : (q + 1) * p.depth] = up[q * p.out : (q + 1) * p.out, :]
    mlp_pack[:, 2 * p.depth :] = down[...]
    for k in range(p.basis):
        u, v = k // p.group, k % p.group
        block[u * p.depth : (u + 1) * p.depth, v * p.out : (v + 1) * p.out] = mix[k]
    used = p.group * p.out
    if p.mix_lanes > used:
        block[:, used:] = jnp.zeros((p.mix_rows, p.mix_lanes - used), BF)
    for row, lane, at, column, count in folds(p):
        mix_pack[row : row + count, lane : lane + 128] = block[
            at : at + count, column : column + 128
        ]


def pack_weights(plan, mix, up, down):
    p = plan
    return pl.pallas_call(
        lambda *refs: pack_kernel(p, *refs),
        out_shape=[
            shape_of((p.out, p.mlp_lanes), BF),
            shape_of((p.fold, p.mlp_lanes), BF),
        ],
        in_specs=whole(3),
        out_specs=whole(2),
        scratch_shapes=[pltpu.VMEM((p.mix_rows, p.mix_lanes), BF)],
        compiler_params=params(60),
        name="pack_weights",
    )(mix, up, down)


def sources(z):
    return z, z ^ 3, z ^ 1, z ^ 2


def contract_kernel(plan, own, far, both, *rest):
    p = plan
    pieces = rest[: p.lats]
    contracted, grid, taps, numbers, table, done = rest[p.lats :]
    a, z, x = place()
    even = x == 0
    for s in range(p.lats):
        for g in range(p.groups):
            lo = p.body + 16 * g
            block = pieces[s][lo : lo + 16, :].astype(F32)
            for i in range(p.taps_row):
                if g * p.taps_row + i < p.cycles:
                    taps[s * p.cycles + g * p.taps_row + i] = block[:, i * 128 : (i + 1) * 128]
            numbers[8 * (s * p.groups + g) : 8 * (s * p.groups + g) + 8, :] = block[
                8:16, :
            ].astype(jnp.int32)
    load = pltpu.make_async_copy(numbers, table, done)
    load.start()
    edge = jnp.zeros((HREACH,) + grid.shape[1:], BF)
    grid[0:HREACH] = edge
    grid[HREACH + p.total : 2 * HREACH + p.total] = edge
    gap = p.kpad - p.depth
    for s in range(p.lats):
        band = lax.rem(a - s + p.lats, p.lats)
        lo = s * p.body

        def read(ref, start=0):
            at = start + lo
            return ref[at : at + p.body, 0 : p.lanes].astype(F32)

        mine, other = read(own), read(both)
        first, second = read(both, p.lats * p.body), read(far)
        blocks = (
            jnp.where(even, first, second),
            jnp.where(even, mine, other),
            jnp.where(even, other, mine),
            jnp.where(even, second, first),
        )
        joined = jnp.concatenate(
            [block.reshape(p.cycles, p.cells, p.lanes) for block in blocks], axis=1
        ).astype(BF)
        where = HREACH + band * p.cycles
        for e in range(p.members):
            grid[pl.ds(where, p.cycles), :, e * p.kpad : e * p.kpad + p.depth] = joined[
                :, :, e * p.depth : (e + 1) * p.depth
            ]
            if gap:
                grid[pl.ds(where, p.cycles), :, e * p.kpad + p.depth : (e + 1) * p.kpad] = (
                    jnp.zeros((p.cycles, p.window, gap), BF)
                )
    load.wait()

    for s in range(p.lats):
        band = lax.rem(a - s + p.lats, p.lats)
        for c in range(p.cycles):
            i = band * p.cycles + c
            line = 8 * (s * p.groups + c // p.taps_row) + p.basis - 8
            lane = (c % p.taps_row) * 128
            source = jnp.concatenate(
                [grid[i + HREACH + table[line, lane + r]] for r in range(p.slots)], axis=0
            )
            lhs = jnp.concatenate(
                [
                    pltpu.roll(
                        jnp.broadcast_to(
                            taps[s * p.cycles + c, k : k + 1, :], (p.double, 128)
                        ),
                        0,
                        1,
                        stride=1,
                        stride_axis=0,
                    )
                    for k in range(p.basis)
                ],
                axis=0,
            ).astype(BF)
            result = jnp.dot(lhs, source, preferred_element_type=F32).astype(BF)
            at = i * (p.members * p.double)
            for e in range(p.members):
                for k in range(p.basis):
                    contracted[
                        pl.ds(pl.multiple_of(at + e * p.double, p.double), p.double),
                        k * p.kpad : (k + 1) * p.kpad,
                    ] = result[
                        k * p.double : (k + 1) * p.double, e * p.kpad : (e + 1) * p.kpad
                    ]


def contract(plan, own, far, both, pieces):
    p = plan
    lines = 8 * p.lats * p.groups
    return pl.pallas_call(
        lambda *refs: contract_kernel(p, *refs),
        out_shape=shape_of((p.total * p.members * p.double, p.basis * p.kpad), BF),
        in_specs=whole(3 + p.lats),
        out_specs=pl.BlockSpec(memory_space=pltpu.VMEM),
        scratch_shapes=[
            pltpu.VMEM((p.total + 2 * HREACH, p.window, p.members * p.kpad), BF),
            pltpu.VMEM((p.total, 16, 128), F32),
            pltpu.VMEM((lines, p.wide), jnp.int32),
            pltpu.SMEM((lines, p.wide), jnp.int32),
            pltpu.SemaphoreType.DMA,
        ],
        compiler_params=params(),
        name="contract",
    )(own, far, both, *pieces)


def mix_kernel(plan, contracted, *rest):
    p = plan
    packs = rest[:4]
    keep, send, slots, mixing = rest[4:]
    a, z, x = place()
    if p.kpad > p.depth:
        for k in range(p.basis):
            mixing[k * p.kpad + p.depth : (k + 1) * p.kpad, :] = jnp.zeros(
                (p.kpad - p.depth, p.zs * p.out), BF
            )
    for ref, source in zip(packs, sources(z)):
        top = ref.shape[0] - p.fold
        for row, lane, at, column, count in folds(p):
            slots[source, at : at + count, column : column + 128] = ref[
                top + row : top + row + count, lane : lane + 128
            ]
    for b in range(p.zs):
        for k in range(p.basis):
            u, v = k // p.group, k % p.group
            mixing[k * p.kpad : k * p.kpad + p.depth, b * p.out : (b + 1) * p.out] = slots[
                b, u * p.depth : (u + 1) * p.depth, v * p.out : (v + 1) * p.out
            ]
    count = 2 * p.half
    core = lax.rem(a, 2)
    for t in range(p.ys):
        y = lax.rem(a // 2 + t, p.ys)
        for mate in range(2):
            band = 2 * y + (core if mate == 0 else 1 - core)
            at = pl.multiple_of(band * count, count)
            total = jnp.dot(
                contracted[pl.ds(at, count), :], mixing[...], preferred_element_type=F32
            ).reshape(p.cycles * p.members, 2, p.cells, p.zs * p.out)
            left = total[:, 0].reshape(p.half, p.zs * p.out)
            right = total[:, 1].reshape(p.half, p.zs * p.out)
            for w in range(2):
                value = jnp.where((x ^ w) == 0, left, right)
                if mate == 0:
                    keep[2 * t + w] = value
                else:
                    send[2 * t + w] = value.astype(BF)


def mix_basis(plan, contracted, packs):
    p = plan
    out = p.zs * p.out
    return pl.pallas_call(
        lambda *refs: mix_kernel(p, *refs),
        out_shape=[
            shape_of((2 * p.ys, p.half, out), F32),
            shape_of((2 * p.ys, p.half, out), BF),
        ],
        in_specs=whole(5),
        out_specs=whole(2),
        scratch_shapes=[
            pltpu.VMEM((p.zs, p.mix_rows, p.mix_lanes), BF),
            pltpu.VMEM((p.basis * p.kpad, out), BF),
        ],
        compiler_params=params(),
        name="mix_basis",
    )(contracted, *packs)


def add_kernel(keep, arrived, own, *msgs):
    for i in range(keep.shape[0]):
        value = keep[i] + arrived[i].astype(F32)
        if i == 0:
            own[...] = value
        else:
            msgs[i - 1][...] = value.astype(BF)


def add_cores(keep, arrived):
    count, half, out = keep.shape
    outs = pl.pallas_call(
        add_kernel,
        out_shape=[shape_of((half, out), F32)] + [shape_of((half, out), BF)] * (count - 1),
        in_specs=whole(2),
        out_specs=whole(count),
        compiler_params=params(),
        name="add_cores",
    )(keep, arrived)
    return outs[0], outs[1:]


def unpack_kernel(plan, mine, sibling, up, down, slots):
    p = plan
    a, z, x = place()
    core = lax.rem(a, 2)
    for mate, stack in enumerate((mine, sibling)):
        c = core if mate == 0 else 1 - core
        for step in range(4):
            low, high = step % 2, step // 2
            dx = jnp.where(c == 0, low, high)
            dy = jnp.where(c == 0, high, low)
            lat = 2 * ((a // 2) ^ dy) + c
            for s, source in enumerate(sources(z)):
                lon = 2 * source + (x ^ dx)
                index = step * p.zs + s
                slots[lat * p.lons + lon] = stack[index * p.out : (index + 1) * p.out, :]
    for a in range(p.lats):
        for b in range(p.lons):
            i = a * p.lons + b
            for q in range(p.lift // p.out):
                up[
                    a * p.depth + q * p.out : a * p.depth + (q + 1) * p.out,
                    b * p.lift : (b + 1) * p.lift,
                ] = slots[i, :, q * p.depth : (q + 1) * p.depth]
            down[
                b * p.out : (b + 1) * p.out, a * p.down_rows : (a + 1) * p.down_rows
            ] = slots[i, :, 2 * p.depth :]


def unpack(plan, mine, sibling):
    p = plan
    return pl.pallas_call(
        lambda *refs: unpack_kernel(p, *refs),
        out_shape=[
            shape_of((p.lats * p.depth, p.lons * p.lift), BF),
            shape_of((p.lons * p.out, p.lats * p.down_rows), BF),
        ],
        in_specs=whole(2),
        out_specs=whole(2),
        scratch_shapes=[pltpu.VMEM((p.lats * p.lons, p.out, p.mlp_lanes), BF)],
        compiler_params=params(),
        name="mlp_weights",
    )(mine, sibling)


def mlp_kernel(plan, latent, bias, up, down, own, *rest):
    p = plan
    arrived, (out, conv) = rest[:-2], rest[-2:]
    _, _, x = place()
    even = x == 0
    mine = own[...]
    other = None
    for i, ref in enumerate(arrived):
        value = ref[...].astype(F32)
        if (i + 1) % 2 == 0:
            mine = mine + value
        else:
            other = value if other is None else other + value
    first = jnp.where(even, mine, other)
    second = jnp.where(even, other, mine)
    for b in range(p.zs):
        cols = slice(b * p.out, (b + 1) * p.out)
        conv[:, 2 * b * p.out : (2 * b + 1) * p.out] = first[:, cols]
        conv[:, (2 * b + 1) * p.out : (2 * b + 2) * p.out] = second[:, cols]
    hidden = (latent[...].astype(F32).reshape(p.half, p.width) + conv[...]).astype(BF)
    lifted = jnp.dot(hidden, up[...], preferred_element_type=F32) + bias[...]
    activated = (lifted * (1.0 + lax.erf(lifted * (0.5**0.5))) * 0.5).astype(BF)
    lowered = lax.dot_general(
        activated, down[...], (((1,), (1,)), ((), ())), preferred_element_type=F32
    )
    out[...] = (hidden.astype(F32) + lowered).astype(BF).reshape(out.shape)


def mlp(plan, latent, bias, up, down, own, arrived):
    p = plan
    return pl.pallas_call(
        lambda *refs: mlp_kernel(p, *refs),
        out_shape=shape_of(latent.shape, BF),
        in_specs=whole(5 + len(arrived)),
        out_specs=pl.BlockSpec(memory_space=pltpu.VMEM),
        scratch_shapes=[pltpu.VMEM((p.half, p.width), F32)],
        compiler_params=params(),
        name="sum_mlp",
    )(latent, bias, up, down, own, *arrived)


def mover(plan):
    p = plan

    def move(value, target):
        pairs = []
        for a in range(p.lats):
            for b in range(p.lons):
                c, d = target(a, b)
                pairs.append((a * p.lons + b, (c % p.lats) * p.lons + d % p.lons))
        return lax.ppermute(value, AXES, pairs)

    return move


def after(value, *others):
    return lax.optimization_barrier((value,) + others)[0]


def shards_fast(
    plan,
    latent,
    norm_gain,
    filters,
    row_offsets,
    col_offsets,
    mix_weight,
    up_weight,
    up_bias,
    down_weight,
):
    p = plan
    move = mover(p)
    taps = filters.transpose(1, 2, 3, 0).reshape(p.cycles, p.slots * p.band, p.basis)
    msgs = normal_pieces(
        p, row_offsets.T, col_offsets.T, latent, norm_gain, taps
    )
    pieces = [msgs[0]]
    for s in range(1, p.lats):
        pieces.append(move(msgs[s], lambda i, j, s=s: (i + s, j)))
    mlp_pack, mix_pack = pack_weights(
        p, mix_weight, after(up_weight, msgs[0]), down_weight.T
    )

    def mirror(i, j):
        return i, 2 * (p.zs - 1) - 2 * (j // 2) + j % 2

    def beside(i, j):
        return i, j ^ 2

    turned = move(mix_pack, mirror)
    last = move(turned, beside)

    own = jnp.concatenate([piece[: p.body] for piece in pieces], axis=0)
    far = move(own, lambda i, j: (i, j + 2 if j % 2 else j - 2))
    both = move(jnp.concatenate([own, far], axis=0), lambda i, j: (i, j ^ 1))
    contracted = contract(p, own, far, both, pieces)

    near = jnp.concatenate([mlp_pack, move(mlp_pack, mirror), mix_pack], axis=0)
    next_to = move(after(near, far), beside)
    packs = [mix_pack, turned, next_to, last]
    share = jnp.concatenate([near[: 2 * p.out], next_to[: 2 * p.out]], axis=0)
    share = after(share, both, turned)
    crossed = move(share, lambda i, j: (i + 2, j) if i % 2 else (i, j ^ 1))
    share = after(jnp.concatenate([share, crossed], axis=0), last, contracted)
    crossed = move(share, lambda i, j: (i, j ^ 1) if i % 2 else (i + 2, j))
    keep, send = mix_basis(p, contracted, packs)
    arrived = move(send, lambda i, j: (i ^ 1, j))
    mine, outgoing = add_cores(keep, arrived)
    incoming = []
    for index, value in enumerate(outgoing):
        t, w = (index + 1) // 2, (index + 1) % 2
        incoming.append(move(value, lambda i, j, t=t, w=w: (i + 2 * t, j ^ w)))

    share = after(jnp.concatenate([share, crossed], axis=0), incoming[0])
    up, down = unpack(p, share, move(share, lambda i, j: (i ^ 1, j)))
    return mlp(p, latent, up_bias, up, down, mine, incoming)


def padded(shard, sides, width, wrap):
    for axis, dim in sides:
        size, length = (lax.axis_size(axis), shard.shape[dim])
        up = [(i, (i + 1) % size) for i in range(size if wrap else size - 1)]
        down = [(j, i) for i, j in up]
        last = lax.slice_in_dim(shard, length - width, length, axis=dim)
        leading = lax.slice_in_dim(shard, 0, width, axis=dim)
        before = lax.ppermute(last, axis, up)
        after = lax.ppermute(leading, axis, down)
        shard = jnp.concatenate([before, shard, after], axis=dim)
    return shard


def normalize(latent, norm_gain):
    widened = latent.astype(jnp.float32)
    channel_mean = jnp.mean(widened, axis=-1, keepdims=True)
    centered = widened - channel_mean
    variance = jnp.mean(centered * centered, axis=-1, keepdims=True)
    return (centered * lax.rsqrt(variance + EPSILON) * norm_gain).astype(jnp.bfloat16)


def contract_cycles(
    band_slab, filters, row_offsets, col_offsets, cycle_count, out_cells, shift_cells
):
    members = band_slab.shape[1]
    channel_share = band_slab.shape[3]

    def cycle_output(cycle_index):
        pieces = []
        for row_slot in range(R):
            where = cycle_index + HREACH + row_offsets[cycle_index, row_slot]
            source = lax.dynamic_index_in_dim(band_slab, where, 0, keepdims=False)
            start = col_offsets[cycle_index, row_slot] + shift_cells
            segment = lax.dynamic_slice_in_dim(source, start, out_cells + BW - 1, 1)
            for band_step in range(BW):
                pieces.append(segment[:, band_step : band_step + out_cells])
        stacked = jnp.stack(pieces).reshape(R * BW, members * out_cells * channel_share)
        cycle_filter = lax.dynamic_index_in_dim(filters, cycle_index, 1, keepdims=False).reshape(
            KB, R * BW
        )
        contracted = jnp.dot(cycle_filter, stacked, preferred_element_type=jnp.float32).astype(
            jnp.bfloat16
        )
        return contracted.reshape(KB, members, out_cells, channel_share)

    return lax.map(cycle_output, jnp.arange(cycle_count, dtype=jnp.int32))


def shards_plain(
    latent,
    norm_gain,
    filters,
    row_offsets,
    col_offsets,
    mix_weight,
    up_weight,
    up_bias,
    down_weight,
):
    cycle_count = latent.shape[0]
    local_cells = latent.shape[2]
    width = latent.shape[3]
    partial_weights = (
        lax.all_gather(mix_weight, "lat", axis=1, tiled=True),
        lax.all_gather(up_weight, "lat", axis=0, tiled=True),
        lax.all_gather(down_weight, "lat", axis=0, tiled=True),
    )
    mix_full, up_full, down_full = (
        lax.all_gather(partial_weights[0], "lon", axis=2, tiled=True),
        lax.all_gather(partial_weights[1], "lon", axis=1, tiled=True),
        lax.all_gather(partial_weights[2], "lon", axis=1, tiled=True),
    )
    normalized = normalize(latent, norm_gain)
    side_reach = BW // 2 + 2
    cycle_rims = padded(normalized, (("lat", 0),), HREACH, False)
    band_slab = padded(cycle_rims, (("lon", 2),), side_reach, True)
    contracted = contract_cycles(
        band_slab, filters, row_offsets, col_offsets, cycle_count, local_cells, side_reach
    )
    convolved = jnp.einsum(
        "ikejc,kcd->iejd", contracted, mix_full, preferred_element_type=jnp.float32
    )
    hidden = (latent.astype(jnp.float32) + convolved).astype(jnp.bfloat16)
    flattened = hidden.reshape(-1, width)
    lifted = jnp.dot(flattened, up_full, preferred_element_type=jnp.float32) + up_bias
    activated = jax.nn.gelu(lifted, approximate=False).astype(jnp.bfloat16)
    result = flattened.astype(jnp.float32) + jnp.dot(
        activated, down_full, preferred_element_type=jnp.float32
    )
    return result.astype(jnp.bfloat16).reshape(latent.shape)


def solution(mesh):
    lats, lons = mesh.shape["lat"], mesh.shape["lon"]

    def shards(*args):
        latent, _, filters, _, _, mix_weight, up_weight, _, down_weight = args
        plan = Plan(lats, lons, latent, filters, mix_weight, up_weight, down_weight)
        if plan.fits():
            return shards_fast(plan, *args)
        return shards_plain(*args)

    in_specs = (
        P("lat", None, "lon", None),
        P(),
        P(None, "lat", None, None),
        P("lat", None),
        P("lat", None),
        P(None, "lat", "lon"),
        P("lat", "lon"),
        P(),
        P("lat", "lon"),
    )
    out_specs = P("lat", None, "lon", None)
    return jax.shard_map(shards, mesh=mesh, in_specs=in_specs, out_specs=out_specs, check_vma=False)
```

```python
import jax
import jax.numpy as jnp
from jax import lax
from jax.experimental import pallas as pl
from jax.experimental.pallas import tpu as pltpu
from jax.sharding import PartitionSpec as P

HREACH = 2
KB = 9
R = 4
BW = 8
EPSILON = 1e-05
BF = jnp.bfloat16
F32 = jnp.float32
AXES = ("lat", "lon")


def shape_of(shape, dtype):
    return jax.ShapeDtypeStruct(tuple(shape), dtype)


def whole(count):
    return [pl.BlockSpec(memory_space=pltpu.VMEM) for _ in range(count)]


def scalars(count):
    return [pl.BlockSpec(memory_space=pltpu.SMEM) for _ in range(count)]


def params(mebibytes=24):
    return pltpu.CompilerParams(vmem_limit_bytes=mebibytes * 1024 * 1024)


class Plan:
    def __init__(self, lats, lons, latent, filters, mix_weight, up_weight, down_weight):
        self.lats, self.lons = lats, lons
        self.ys = lats // 2
        self.zs = lons // 2
        self.cycles, self.members, self.cells, self.width = latent.shape
        self.basis, _, self.slots, self.band = filters.shape
        self.depth, self.out = mix_weight.shape[1], mix_weight.shape[2]
        self.lift = up_weight.shape[1]
        self.down_rows = down_weight.shape[0]
        self.half = self.cycles * self.members * self.cells
        self.body = self.cycles * self.cells
        self.lanes = self.members * self.depth
        self.wide = -(-self.lanes // 128) * 128
        self.taps_row = self.wide // 128
        self.groups = -(-self.cycles // self.taps_row)
        self.piece = self.body + 16 * self.groups
        self.kpad = -(-self.depth // 128) * 128
        self.group = 3
        self.mix_rows = (self.basis // 3) * self.depth
        self.mix_lanes = 256
        self.fold = 2 * self.mix_rows // 5
        self.mlp_lanes = 8 * self.out
        self.total = self.cycles * lats
        self.window = 4 * self.cells
        self.double = 2 * self.cells

    def fits(self):
        return (
            self.lats == 4
            and self.zs == 4
            and self.cells == 8
            and self.members == 2
            and self.slots * self.window == 128
            and self.band == 8
            and self.basis % 3 == 0
            and self.basis < 16
            and self.lift == 2 * self.out
            and self.depth == self.lift
            and self.down_rows == 4 * self.out
            and self.out % 16 == 0
            and self.mlp_lanes == 5 * 128
            and 3 * self.out <= self.mix_lanes
            and self.fold % 32 == 0
            and 5 * self.fold == 2 * self.mix_rows
            and self.body % 16 == 0
        )


def folds(plan):
    p = plan
    places = []
    for c in range(2):
        for h in range(2):
            places.append((0, (2 * c + h) * 128, h * p.fold, c * 128, p.fold))
        places.append((c * (p.fold // 2), 512, 2 * p.fold, c * 128, p.fold // 2))
    return places


def place():
    a, b = lax.axis_index("lat"), lax.axis_index("lon")
    return a, b // 2, b % 2


def normal_kernel(plan, rows, cols, latent, gain, filters, *rest):
    p = plan
    msgs, stage = rest[: p.lats], rest[p.lats]
    a, _, _ = place()
    flat = latent[...].astype(F32).reshape(p.half, p.width)
    mean = jnp.mean(flat, axis=-1, keepdims=True)
    centered = flat - mean
    variance = jnp.mean(centered * centered, axis=-1, keepdims=True)
    normal = centered * lax.rsqrt(variance + EPSILON) * gain[...]
    normal = normal.reshape(p.cycles, p.members, p.cells, p.width)
    for e in range(p.members):
        part = normal[:, e].reshape(p.body, p.width).astype(BF)
        for q in range(p.lats):
            slot = lax.rem(q - a + p.lats, p.lats)
            stage[slot, :, e * p.depth : (e + 1) * p.depth] = part[
                :, q * p.depth : (q + 1) * p.depth
            ]
    row = lax.broadcasted_iota(jnp.int32, (p.slots * p.band, 128), 0)
    lane = lax.broadcasted_iota(jnp.int32, (p.slots * p.band, 128), 1)
    first = lax.broadcasted_iota(jnp.int32, (16, 128), 0)
    second = lax.broadcasted_iota(jnp.int32, (16, 128), 1)
    tails = []
    for g in range(p.groups):
        blocks = []
        for i in range(g * p.taps_row, (g + 1) * p.taps_row):
            if i >= p.cycles:
                blocks.append(jnp.zeros((16, 128), F32))
                continue
            target = jnp.zeros((p.slots * p.band, 128), jnp.int32)
            offset = jnp.zeros((16, 128), jnp.int32)
            for r in range(p.slots):
                start = r * p.window + p.cells + cols[r, i] - r * p.band
                target = jnp.where(row // p.band == r, start + row, target)
                offset = jnp.where(second == r, rows[r, i], offset)
            hit = jnp.where(lane == target, 1.0, 0.0).astype(BF)
            taps = lax.dot_general(
                filters[i], hit, (((0,), (0,)), ((), ())), preferred_element_type=F32
            )
            taps = jnp.concatenate([taps, jnp.zeros((16 - p.basis, 128), F32)], axis=0)
            blocks.append(jnp.where(first == p.basis, offset.astype(F32), taps))
        tails.append(jnp.concatenate(blocks, axis=1).astype(BF))
    for s in range(p.lats):
        msgs[s][0 : p.body, 0 : p.lanes] = stage[s]
        if p.wide > p.lanes:
            msgs[s][0 : p.body, p.lanes :] = jnp.zeros((p.body, p.wide - p.lanes), BF)
        for g in range(p.groups):
            msgs[s][p.body + 16 * g : p.body + 16 * (g + 1), :] = tails[g]


def normal_pieces(plan, rows, cols, latent, gain, filters):
    p = plan
    return pl.pallas_call(
        lambda *refs: normal_kernel(p, *refs),
        out_shape=[shape_of((p.piece, p.wide), BF)] * p.lats,
        in_specs=scalars(2) + whole(3),
        out_specs=whole(p.lats),
        scratch_shapes=[pltpu.VMEM((p.lats, p.body, p.lanes), BF)],
        compiler_params=params(60),
        name="normalize",
    )(rows, cols, latent, gain, filters)


def pack_kernel(plan, mix, up, down, mlp_pack, mix_pack, block):
    p = plan
    for q in range(p.lift // p.out):
        mlp_pack[:, q * p.depth : (q + 1) * p.depth] = up[q * p.out : (q + 1) * p.out, :]
    mlp_pack[:, 2 * p.depth :] = down[...]
    for k in range(p.basis):
        u, v = k // p.group, k % p.group
        block[u * p.depth : (u + 1) * p.depth, v * p.out : (v + 1) * p.out] = mix[k]
    used = p.group * p.out
    if p.mix_lanes > used:
        block[:, used:] = jnp.zeros((p.mix_rows, p.mix_lanes - used), BF)
    for row, lane, at, column, count in folds(p):
        mix_pack[row : row + count, lane : lane + 128] = block[
            at : at + count, column : column + 128
        ]


def pack_weights(plan, mix, up, down):
    p = plan
    return pl.pallas_call(
        lambda *refs: pack_kernel(p, *refs),
        out_shape=[
            shape_of((p.out, p.mlp_lanes), BF),
            shape_of((p.fold, p.mlp_lanes), BF),
        ],
        in_specs=whole(3),
        out_specs=whole(2),
        scratch_shapes=[pltpu.VMEM((p.mix_rows, p.mix_lanes), BF)],
        compiler_params=params(60),
        name="pack_weights",
    )(mix, up, down)


def sources(z):
    return z, z ^ 3, z ^ 1, z ^ 2


def contract_kernel(plan, own, far, both, *rest):
    p = plan
    pieces = rest[: p.lats]
    contracted, grid, taps, numbers, table, done = rest[p.lats :]
    a, z, x = place()
    even = x == 0
    for s in range(p.lats):
        for g in range(p.groups):
            lo = p.body + 16 * g
            block = pieces[s][lo : lo + 16, :].astype(F32)
            for i in range(p.taps_row):
                if g * p.taps_row + i < p.cycles:
                    taps[s * p.cycles + g * p.taps_row + i] = block[:, i * 128 : (i + 1) * 128]
            numbers[8 * (s * p.groups + g) : 8 * (s * p.groups + g) + 8, :] = block[
                8:16, :
            ].astype(jnp.int32)
    load = pltpu.make_async_copy(numbers, table, done)
    load.start()
    edge = jnp.zeros((HREACH,) + grid.shape[1:], BF)
    grid[0:HREACH] = edge
    grid[HREACH + p.total : 2 * HREACH + p.total] = edge
    gap = p.kpad - p.depth
    for s in range(p.lats):
        band = lax.rem(a - s + p.lats, p.lats)
        lo = s * p.body

        def read(ref, start=0):
            at = start + lo
            return ref[at : at + p.body, 0 : p.lanes].astype(F32)

        mine, other = read(own), read(both)
        first, second = read(both, p.lats * p.body), read(far)
        blocks = (
            jnp.where(even, first, second),
            jnp.where(even, mine, other),
            jnp.where(even, other, mine),
            jnp.where(even, second, first),
        )
        joined = jnp.concatenate(
            [block.reshape(p.cycles, p.cells, p.lanes) for block in blocks], axis=1
        ).astype(BF)
        where = HREACH + band * p.cycles
        for e in range(p.members):
            grid[pl.ds(where, p.cycles), :, e * p.kpad : e * p.kpad + p.depth] = joined[
                :, :, e * p.depth : (e + 1) * p.depth
            ]
            if gap:
                grid[pl.ds(where, p.cycles), :, e * p.kpad + p.depth : (e + 1) * p.kpad] = (
                    jnp.zeros((p.cycles, p.window, gap), BF)
                )
    load.wait()

    for s in range(p.lats):
        band = lax.rem(a - s + p.lats, p.lats)
        for c in range(p.cycles):
            i = band * p.cycles + c
            line = 8 * (s * p.groups + c // p.taps_row) + p.basis - 8
            lane = (c % p.taps_row) * 128
            source = jnp.concatenate(
                [grid[i + HREACH + table[line, lane + r]] for r in range(p.slots)], axis=0
            )
            lhs = jnp.concatenate(
                [
                    pltpu.roll(
                        jnp.broadcast_to(
                            taps[s * p.cycles + c, k : k + 1, :], (p.double, 128)
                        ),
                        0,
                        1,
                        stride=1,
                        stride_axis=0,
                    )
                    for k in range(p.basis)
                ],
                axis=0,
            ).astype(BF)
            result = jnp.dot(lhs, source, preferred_element_type=F32).astype(BF)
            at = i * (p.members * p.double)
            for e in range(p.members):
                for k in range(p.basis):
                    contracted[
                        pl.ds(pl.multiple_of(at + e * p.double, p.double), p.double),
                        k * p.kpad : (k + 1) * p.kpad,
                    ] = result[
                        k * p.double : (k + 1) * p.double, e * p.kpad : (e + 1) * p.kpad
                    ]


def contract(plan, own, far, both, pieces):
    p = plan
    lines = 8 * p.lats * p.groups
    return pl.pallas_call(
        lambda *refs: contract_kernel(p, *refs),
        out_shape=shape_of((p.total * p.members * p.double, p.basis * p.kpad), BF),
        in_specs=whole(3 + p.lats),
        out_specs=pl.BlockSpec(memory_space=pltpu.VMEM),
        scratch_shapes=[
            pltpu.VMEM((p.total + 2 * HREACH, p.window, p.members * p.kpad), BF),
            pltpu.VMEM((p.total, 16, 128), F32),
            pltpu.VMEM((lines, p.wide), jnp.int32),
            pltpu.SMEM((lines, p.wide), jnp.int32),
            pltpu.SemaphoreType.DMA,
        ],
        compiler_params=params(),
        name="contract",
    )(own, far, both, *pieces)


def mix_kernel(plan, contracted, *rest):
    p = plan
    packs = rest[:4]
    keep, send, slots, mixing = rest[4:]
    a, z, x = place()
    if p.kpad > p.depth:
        for k in range(p.basis):
            mixing[k * p.kpad + p.depth : (k + 1) * p.kpad, :] = jnp.zeros(
                (p.kpad - p.depth, p.zs * p.out), BF
            )
    for ref, source in zip(packs, sources(z)):
        top = ref.shape[0] - p.fold
        for row, lane, at, column, count in folds(p):
            slots[source, at : at + count, column : column + 128] = ref[
                top + row : top + row + count, lane : lane + 128
            ]
    for b in range(p.zs):
        for k in range(p.basis):
            u, v = k // p.group, k % p.group
            mixing[k * p.kpad : k * p.kpad + p.depth, b * p.out : (b + 1) * p.out] = slots[
                b, u * p.depth : (u + 1) * p.depth, v * p.out : (v + 1) * p.out
            ]
    count = 2 * p.half
    core = lax.rem(a, 2)
    for t in range(p.ys):
        y = lax.rem(a // 2 + t, p.ys)
        for mate in range(2):
            band = 2 * y + (core if mate == 0 else 1 - core)
            at = pl.multiple_of(band * count, count)
            total = jnp.dot(
                contracted[pl.ds(at, count), :], mixing[...], preferred_element_type=F32
            ).reshape(p.cycles * p.members, 2, p.cells, p.zs * p.out)
            left = total[:, 0].reshape(p.half, p.zs * p.out)
            right = total[:, 1].reshape(p.half, p.zs * p.out)
            for w in range(2):
                value = jnp.where((x ^ w) == 0, left, right)
                if mate == 0:
                    keep[2 * t + w] = value
                else:
                    send[2 * t + w] = value.astype(BF)


def mix_basis(plan, contracted, packs):
    p = plan
    out = p.zs * p.out
    return pl.pallas_call(
        lambda *refs: mix_kernel(p, *refs),
        out_shape=[
            shape_of((2 * p.ys, p.half, out), F32),
            shape_of((2 * p.ys, p.half, out), BF),
        ],
        in_specs=whole(5),
        out_specs=whole(2),
        scratch_shapes=[
            pltpu.VMEM((p.zs, p.mix_rows, p.mix_lanes), BF),
            pltpu.VMEM((p.basis * p.kpad, out), BF),
        ],
        compiler_params=params(),
        name="mix_basis",
    )(contracted, *packs)


def add_kernel(keep, arrived, own, *msgs):
    for i in range(keep.shape[0]):
        value = keep[i] + arrived[i].astype(F32)
        if i == 0:
            own[...] = value
        else:
            msgs[i - 1][...] = value.astype(BF)


def add_cores(keep, arrived):
    count, half, out = keep.shape
    outs = pl.pallas_call(
        add_kernel,
        out_shape=[shape_of((half, out), F32)] + [shape_of((half, out), BF)] * (count - 1),
        in_specs=whole(2),
        out_specs=whole(count),
        compiler_params=params(),
        name="add_cores",
    )(keep, arrived)
    return outs[0], outs[1:]


def unpack_kernel(plan, mine, sibling, up, down, slots):
    p = plan
    a, z, x = place()
    core = lax.rem(a, 2)
    for mate, stack in enumerate((mine, sibling)):
        c = core if mate == 0 else 1 - core
        for step in range(4):
            low, high = step % 2, step // 2
            dx = jnp.where(c == 0, low, high)
            dy = jnp.where(c == 0, high, low)
            lat = 2 * ((a // 2) ^ dy) + c
            for s, source in enumerate(sources(z)):
                lon = 2 * source + (x ^ dx)
                index = step * p.zs + s
                slots[lat * p.lons + lon] = stack[index * p.out : (index + 1) * p.out, :]
    for a in range(p.lats):
        for b in range(p.lons):
            i = a * p.lons + b
            for q in range(p.lift // p.out):
                up[
                    a * p.depth + q * p.out : a * p.depth + (q + 1) * p.out,
                    b * p.lift : (b + 1) * p.lift,
                ] = slots[i, :, q * p.depth : (q + 1) * p.depth]
            down[
                b * p.out : (b + 1) * p.out, a * p.down_rows : (a + 1) * p.down_rows
            ] = slots[i, :, 2 * p.depth :]


def unpack(plan, mine, sibling):
    p = plan
    return pl.pallas_call(
        lambda *refs: unpack_kernel(p, *refs),
        out_shape=[
            shape_of((p.lats * p.depth, p.lons * p.lift), BF),
            shape_of((p.lons * p.out, p.lats * p.down_rows), BF),
        ],
        in_specs=whole(2),
        out_specs=whole(2),
        scratch_shapes=[pltpu.VMEM((p.lats * p.lons, p.out, p.mlp_lanes), BF)],
        compiler_params=params(),
        name="mlp_weights",
    )(mine, sibling)


def mlp_kernel(plan, latent, bias, up, down, own, *rest):
    p = plan
    arrived, (out, conv) = rest[:-2], rest[-2:]
    _, _, x = place()
    even = x == 0
    mine = own[...]
    other = None
    for i, ref in enumerate(arrived):
        value = ref[...].astype(F32)
        if (i + 1) % 2 == 0:
            mine = mine + value
        else:
            other = value if other is None else other + value
    first = jnp.where(even, mine, other)
    second = jnp.where(even, other, mine)
    for b in range(p.zs):
        cols = slice(b * p.out, (b + 1) * p.out)
        conv[:, 2 * b * p.out : (2 * b + 1) * p.out] = first[:, cols]
        conv[:, (2 * b + 1) * p.out : (2 * b + 2) * p.out] = second[:, cols]
    hidden = (latent[...].astype(F32).reshape(p.half, p.width) + conv[...]).astype(BF)
    lifted = jnp.dot(hidden, up[...], preferred_element_type=F32) + bias[...]
    activated = (lifted * (1.0 + lax.erf(lifted * (0.5**0.5))) * 0.5).astype(BF)
    lowered = lax.dot_general(
        activated, down[...], (((1,), (1,)), ((), ())), preferred_element_type=F32
    )
    out[...] = (hidden.astype(F32) + lowered).astype(BF).reshape(out.shape)


def mlp(plan, latent, bias, up, down, own, arrived):
    p = plan
    return pl.pallas_call(
        lambda *refs: mlp_kernel(p, *refs),
        out_shape=shape_of(latent.shape, BF),
        in_specs=whole(5 + len(arrived)),
        out_specs=pl.BlockSpec(memory_space=pltpu.VMEM),
        scratch_shapes=[pltpu.VMEM((p.half, p.width), F32)],
        compiler_params=params(),
        name="sum_mlp",
    )(latent, bias, up, down, own, *arrived)


def mover(plan):
    p = plan

    def move(value, target):
        pairs = []
        for a in range(p.lats):
            for b in range(p.lons):
                c, d = target(a, b)
                pairs.append((a * p.lons + b, (c % p.lats) * p.lons + d % p.lons))
        return lax.ppermute(value, AXES, pairs)

    return move


def after(value, *others):
    return lax.optimization_barrier((value,) + others)[0]


def shards_fast(
    plan,
    latent,
    norm_gain,
    filters,
    row_offsets,
    col_offsets,
    mix_weight,
    up_weight,
    up_bias,
    down_weight,
):
    p = plan
    move = mover(p)
    taps = filters.transpose(1, 2, 3, 0).reshape(p.cycles, p.slots * p.band, p.basis)
    msgs = normal_pieces(
        p, row_offsets.T, col_offsets.T, latent, norm_gain, taps
    )
    pieces = [msgs[0]]
    for s in range(1, p.lats):
        pieces.append(move(msgs[s], lambda i, j, s=s: (i + s, j)))
    mlp_pack, mix_pack = pack_weights(
        p, mix_weight, after(up_weight, msgs[0]), down_weight.T
    )

    def mirror(i, j):
        return i, 2 * (p.zs - 1) - 2 * (j // 2) + j % 2

    def beside(i, j):
        return i, j ^ 2

    turned = move(mix_pack, mirror)
    last = move(turned, beside)

    own = jnp.concatenate([piece[: p.body] for piece in pieces], axis=0)
    far = move(own, lambda i, j: (i, j + 2 if j % 2 else j - 2))
    both = move(jnp.concatenate([own, far], axis=0), lambda i, j: (i, j ^ 1))
    contracted = contract(p, own, far, both, pieces)

    near = jnp.concatenate([mlp_pack, move(mlp_pack, mirror), mix_pack], axis=0)
    next_to = move(after(near, far), beside)
    packs = [mix_pack, turned, next_to, last]
    share = jnp.concatenate([near[: 2 * p.out], next_to[: 2 * p.out]], axis=0)
    share = after(share, both)
    crossed = move(share, lambda i, j: (i + 2, j) if i % 2 else (i, j ^ 1))
    share = after(jnp.concatenate([share, crossed], axis=0), turned, contracted)
    crossed = move(share, lambda i, j: (i, j ^ 1) if i % 2 else (i + 2, j))
    keep, send = mix_basis(p, contracted, packs)
    arrived = move(send, lambda i, j: (i ^ 1, j))
    mine, outgoing = add_cores(keep, arrived)
    incoming = []
    for index, value in enumerate(outgoing):
        t, w = (index + 1) // 2, (index + 1) % 2
        incoming.append(move(value, lambda i, j, t=t, w=w: (i + 2 * t, j ^ w)))

    share = after(jnp.concatenate([share, crossed], axis=0), mine)
    up, down = unpack(p, share, move(share, lambda i, j: (i ^ 1, j)))
    return mlp(p, latent, up_bias, up, down, mine, incoming)


def padded(shard, sides, width, wrap):
    for axis, dim in sides:
        size, length = (lax.axis_size(axis), shard.shape[dim])
        up = [(i, (i + 1) % size) for i in range(size if wrap else size - 1)]
        down = [(j, i) for i, j in up]
        last = lax.slice_in_dim(shard, length - width, length, axis=dim)
        leading = lax.slice_in_dim(shard, 0, width, axis=dim)
        before = lax.ppermute(last, axis, up)
        after = lax.ppermute(leading, axis, down)
        shard = jnp.concatenate([before, shard, after], axis=dim)
    return shard


def normalize(latent, norm_gain):
    widened = latent.astype(jnp.float32)
    channel_mean = jnp.mean(widened, axis=-1, keepdims=True)
    centered = widened - channel_mean
    variance = jnp.mean(centered * centered, axis=-1, keepdims=True)
    return (centered * lax.rsqrt(variance + EPSILON) * norm_gain).astype(jnp.bfloat16)


def contract_cycles(
    band_slab, filters, row_offsets, col_offsets, cycle_count, out_cells, shift_cells
):
    members = band_slab.shape[1]
    channel_share = band_slab.shape[3]

    def cycle_output(cycle_index):
        pieces = []
        for row_slot in range(R):
            where = cycle_index + HREACH + row_offsets[cycle_index, row_slot]
            source = lax.dynamic_index_in_dim(band_slab, where, 0, keepdims=False)
            start = col_offsets[cycle_index, row_slot] + shift_cells
            segment = lax.dynamic_slice_in_dim(source, start, out_cells + BW - 1, 1)
            for band_step in range(BW):
                pieces.append(segment[:, band_step : band_step + out_cells])
        stacked = jnp.stack(pieces).reshape(R * BW, members * out_cells * channel_share)
        cycle_filter = lax.dynamic_index_in_dim(filters, cycle_index, 1, keepdims=False).reshape(
            KB, R * BW
        )
        contracted = jnp.dot(cycle_filter, stacked, preferred_element_type=jnp.float32).astype(
            jnp.bfloat16
        )
        return contracted.reshape(KB, members, out_cells, channel_share)

    return lax.map(cycle_output, jnp.arange(cycle_count, dtype=jnp.int32))


def shards_plain(
    latent,
    norm_gain,
    filters,
    row_offsets,
    col_offsets,
    mix_weight,
    up_weight,
    up_bias,
    down_weight,
):
    cycle_count = latent.shape[0]
    local_cells = latent.shape[2]
    width = latent.shape[3]
    partial_weights = (
        lax.all_gather(mix_weight, "lat", axis=1, tiled=True),
        lax.all_gather(up_weight, "lat", axis=0, tiled=True),
        lax.all_gather(down_weight, "lat", axis=0, tiled=True),
    )
    mix_full, up_full, down_full = (
        lax.all_gather(partial_weights[0], "lon", axis=2, tiled=True),
        lax.all_gather(partial_weights[1], "lon", axis=1, tiled=True),
        lax.all_gather(partial_weights[2], "lon", axis=1, tiled=True),
    )
    normalized = normalize(latent, norm_gain)
    side_reach = BW // 2 + 2
    cycle_rims = padded(normalized, (("lat", 0),), HREACH, False)
    band_slab = padded(cycle_rims, (("lon", 2),), side_reach, True)
    contracted = contract_cycles(
        band_slab, filters, row_offsets, col_offsets, cycle_count, local_cells, side_reach
    )
    convolved = jnp.einsum(
        "ikejc,kcd->iejd", contracted, mix_full, preferred_element_type=jnp.float32
    )
    hidden = (latent.astype(jnp.float32) + convolved).astype(jnp.bfloat16)
    flattened = hidden.reshape(-1, width)
    lifted = jnp.dot(flattened, up_full, preferred_element_type=jnp.float32) + up_bias
    activated = jax.nn.gelu(lifted, approximate=False).astype(jnp.bfloat16)
    result = flattened.astype(jnp.float32) + jnp.dot(
        activated, down_full, preferred_element_type=jnp.float32
    )
    return result.astype(jnp.bfloat16).reshape(latent.shape)


def solution(mesh):
    lats, lons = mesh.shape["lat"], mesh.shape["lon"]

    def shards(*args):
        latent, _, filters, _, _, mix_weight, up_weight, _, down_weight = args
        plan = Plan(lats, lons, latent, filters, mix_weight, up_weight, down_weight)
        if plan.fits():
            return shards_fast(plan, *args)
        return shards_plain(*args)

    in_specs = (
        P("lat", None, "lon", None),
        P(),
        P(None, "lat", None, None),
        P("lat", None),
        P("lat", None),
        P(None, "lat", "lon"),
        P("lat", "lon"),
        P(),
        P("lat", "lon"),
    )
    out_specs = P("lat", None, "lon", None)
    return jax.shard_map(shards, mesh=mesh, in_specs=in_specs, out_specs=out_specs, check_vma=False)
```

```python
import jax
import jax.numpy as jnp
from jax import lax
from jax.experimental import pallas as pl
from jax.experimental.pallas import tpu as pltpu
from jax.sharding import PartitionSpec as P

HREACH = 2
KB = 9
R = 4
BW = 8
EPSILON = 1e-05
BF = jnp.bfloat16
F32 = jnp.float32
AXES = ("lat", "lon")


def shape_of(shape, dtype):
    return jax.ShapeDtypeStruct(tuple(shape), dtype)


def whole(count):
    return [pl.BlockSpec(memory_space=pltpu.VMEM) for _ in range(count)]


def scalars(count):
    return [pl.BlockSpec(memory_space=pltpu.SMEM) for _ in range(count)]


def params(mebibytes=24):
    return pltpu.CompilerParams(vmem_limit_bytes=mebibytes * 1024 * 1024)


class Plan:
    def __init__(self, lats, lons, latent, filters, mix_weight, up_weight, down_weight):
        self.lats, self.lons = lats, lons
        self.ys = lats // 2
        self.zs = lons // 2
        self.cycles, self.members, self.cells, self.width = latent.shape
        self.basis, _, self.slots, self.band = filters.shape
        self.depth, self.out = mix_weight.shape[1], mix_weight.shape[2]
        self.lift = up_weight.shape[1]
        self.down_rows = down_weight.shape[0]
        self.half = self.cycles * self.members * self.cells
        self.body = self.cycles * self.cells
        self.lanes = self.members * self.depth
        self.wide = -(-self.lanes // 128) * 128
        self.taps_row = self.wide // 128
        self.groups = -(-self.cycles // self.taps_row)
        self.piece = self.body + 16 * self.groups
        self.kpad = -(-self.depth // 128) * 128
        self.group = 3
        self.mix_rows = (self.basis // 3) * self.depth
        self.mix_lanes = 256
        self.fold = 2 * self.mix_rows // 5
        self.mlp_lanes = 8 * self.out
        self.total = self.cycles * lats
        self.window = 4 * self.cells
        self.double = 2 * self.cells

    def fits(self):
        return (
            self.lats == 4
            and self.zs == 4
            and self.cells == 8
            and self.members == 2
            and self.slots * self.window == 128
            and self.band == 8
            and self.basis % 3 == 0
            and self.basis < 16
            and self.lift == 2 * self.out
            and self.depth == self.lift
            and self.down_rows == 4 * self.out
            and self.out % 16 == 0
            and self.mlp_lanes == 5 * 128
            and 3 * self.out <= self.mix_lanes
            and self.fold % 32 == 0
            and 5 * self.fold == 2 * self.mix_rows
            and self.body % 16 == 0
        )


def folds(plan):
    p = plan
    places = []
    for c in range(2):
        for h in range(2):
            places.append((0, (2 * c + h) * 128, h * p.fold, c * 128, p.fold))
        places.append((c * (p.fold // 2), 512, 2 * p.fold, c * 128, p.fold // 2))
    return places


def place():
    a, b = lax.axis_index("lat"), lax.axis_index("lon")
    return a, b // 2, b % 2


def normal_kernel(plan, rows, cols, latent, gain, filters, *rest):
    p = plan
    msgs, stage = rest[: p.lats], rest[p.lats]
    a, _, _ = place()
    flat = latent[...].astype(F32).reshape(p.half, p.width)
    mean = jnp.mean(flat, axis=-1, keepdims=True)
    centered = flat - mean
    variance = jnp.mean(centered * centered, axis=-1, keepdims=True)
    normal = centered * lax.rsqrt(variance + EPSILON) * gain[...]
    normal = normal.reshape(p.cycles, p.members, p.cells, p.width)
    for e in range(p.members):
        part = normal[:, e].reshape(p.body, p.width).astype(BF)
        for q in range(p.lats):
            slot = lax.rem(q - a + p.lats, p.lats)
            stage[slot, :, e * p.depth : (e + 1) * p.depth] = part[
                :, q * p.depth : (q + 1) * p.depth
            ]
    row = lax.broadcasted_iota(jnp.int32, (p.slots * p.band, 128), 0)
    lane = lax.broadcasted_iota(jnp.int32, (p.slots * p.band, 128), 1)
    first = lax.broadcasted_iota(jnp.int32, (16, 128), 0)
    second = lax.broadcasted_iota(jnp.int32, (16, 128), 1)
    tails = []
    for g in range(p.groups):
        blocks = []
        for i in range(g * p.taps_row, (g + 1) * p.taps_row):
            if i >= p.cycles:
                blocks.append(jnp.zeros((16, 128), F32))
                continue
            target = jnp.zeros((p.slots * p.band, 128), jnp.int32)
            offset = jnp.zeros((16, 128), jnp.int32)
            for r in range(p.slots):
                start = r * p.window + p.cells + cols[r, i] - r * p.band
                target = jnp.where(row // p.band == r, start + row, target)
                offset = jnp.where(second == r, rows[r, i], offset)
            hit = jnp.where(lane == target, 1.0, 0.0).astype(BF)
            taps = lax.dot_general(
                filters[i], hit, (((0,), (0,)), ((), ())), preferred_element_type=F32
            )
            taps = jnp.concatenate([taps, jnp.zeros((16 - p.basis, 128), F32)], axis=0)
            blocks.append(jnp.where(first == p.basis, offset.astype(F32), taps))
        tails.append(jnp.concatenate(blocks, axis=1).astype(BF))
    for s in range(p.lats):
        msgs[s][0 : p.body, 0 : p.lanes] = stage[s]
        if p.wide > p.lanes:
            msgs[s][0 : p.body, p.lanes :] = jnp.zeros((p.body, p.wide - p.lanes), BF)
        for g in range(p.groups):
            msgs[s][p.body + 16 * g : p.body + 16 * (g + 1), :] = tails[g]


def normal_pieces(plan, rows, cols, latent, gain, filters):
    p = plan
    return pl.pallas_call(
        lambda *refs: normal_kernel(p, *refs),
        out_shape=[shape_of((p.piece, p.wide), BF)] * p.lats,
        in_specs=scalars(2) + whole(3),
        out_specs=whole(p.lats),
        scratch_shapes=[pltpu.VMEM((p.lats, p.body, p.lanes), BF)],
        compiler_params=params(60),
        name="normalize",
    )(rows, cols, latent, gain, filters)


def pack_kernel(plan, mix, up, down, mlp_pack, mix_pack, block):
    p = plan
    for q in range(p.lift // p.out):
        mlp_pack[:, q * p.depth : (q + 1) * p.depth] = up[q * p.out : (q + 1) * p.out, :]
    mlp_pack[:, 2 * p.depth :] = down[...]
    for k in range(p.basis):
        u, v = k // p.group, k % p.group
        block[u * p.depth : (u + 1) * p.depth, v * p.out : (v + 1) * p.out] = mix[k]
    used = p.group * p.out
    if p.mix_lanes > used:
        block[:, used:] = jnp.zeros((p.mix_rows, p.mix_lanes - used), BF)
    for row, lane, at, column, count in folds(p):
        mix_pack[row : row + count, lane : lane + 128] = block[
            at : at + count, column : column + 128
        ]


def pack_weights(plan, mix, up, down):
    p = plan
    return pl.pallas_call(
        lambda *refs: pack_kernel(p, *refs),
        out_shape=[
            shape_of((p.out, p.mlp_lanes), BF),
            shape_of((p.fold, p.mlp_lanes), BF),
        ],
        in_specs=whole(3),
        out_specs=whole(2),
        scratch_shapes=[pltpu.VMEM((p.mix_rows, p.mix_lanes), BF)],
        compiler_params=params(60),
        name="pack_weights",
    )(mix, up, down)


def sources(z):
    return z, z ^ 3, z ^ 1, z ^ 2


def contract_kernel(plan, own, far, both, *rest):
    p = plan
    pieces = rest[: p.lats]
    contracted, grid, taps, numbers, table, done = rest[p.lats :]
    a, z, x = place()
    even = x == 0
    for s in range(p.lats):
        for g in range(p.groups):
            lo = p.body + 16 * g
            block = pieces[s][lo : lo + 16, :].astype(F32)
            for i in range(p.taps_row):
                if g * p.taps_row + i < p.cycles:
                    taps[s * p.cycles + g * p.taps_row + i] = block[:, i * 128 : (i + 1) * 128]
            numbers[8 * (s * p.groups + g) : 8 * (s * p.groups + g) + 8, :] = block[
                8:16, :
            ].astype(jnp.int32)
    load = pltpu.make_async_copy(numbers, table, done)
    load.start()
    edge = jnp.zeros((HREACH,) + grid.shape[1:], BF)
    grid[0:HREACH] = edge
    grid[HREACH + p.total : 2 * HREACH + p.total] = edge
    gap = p.kpad - p.depth
    for s in range(p.lats):
        band = lax.rem(a - s + p.lats, p.lats)
        lo = s * p.body

        def read(ref, start=0):
            at = start + lo
            return ref[at : at + p.body, 0 : p.lanes].astype(F32)

        mine, other = read(own), read(both)
        first, second = read(both, p.lats * p.body), read(far)
        blocks = (
            jnp.where(even, first, second),
            jnp.where(even, mine, other),
            jnp.where(even, other, mine),
            jnp.where(even, second, first),
        )
        joined = jnp.concatenate(
            [block.reshape(p.cycles, p.cells, p.lanes) for block in blocks], axis=1
        ).astype(BF)
        where = HREACH + band * p.cycles
        for e in range(p.members):
            grid[pl.ds(where, p.cycles), :, e * p.kpad : e * p.kpad + p.depth] = joined[
                :, :, e * p.depth : (e + 1) * p.depth
            ]
            if gap:
                grid[pl.ds(where, p.cycles), :, e * p.kpad + p.depth : (e + 1) * p.kpad] = (
                    jnp.zeros((p.cycles, p.window, gap), BF)
                )
    load.wait()

    for s in range(p.lats):
        band = lax.rem(a - s + p.lats, p.lats)
        for c in range(p.cycles):
            i = band * p.cycles + c
            line = 8 * (s * p.groups + c // p.taps_row) + p.basis - 8
            lane = (c % p.taps_row) * 128
            source = jnp.concatenate(
                [grid[i + HREACH + table[line, lane + r]] for r in range(p.slots)], axis=0
            )
            lhs = jnp.concatenate(
                [
                    pltpu.roll(
                        jnp.broadcast_to(
                            taps[s * p.cycles + c, k : k + 1, :], (p.double, 128)
                        ),
                        0,
                        1,
                        stride=1,
                        stride_axis=0,
                    )
                    for k in range(p.basis)
                ],
                axis=0,
            ).astype(BF)
            result = jnp.dot(lhs, source, preferred_element_type=F32).astype(BF)
            at = i * (p.members * p.double)
            for e in range(p.members):
                for k in range(p.basis):
                    contracted[
                        pl.ds(pl.multiple_of(at + e * p.double, p.double), p.double),
                        k * p.kpad : (k + 1) * p.kpad,
                    ] = result[
                        k * p.double : (k + 1) * p.double, e * p.kpad : (e + 1) * p.kpad
                    ]


def contract(plan, own, far, both, pieces):
    p = plan
    lines = 8 * p.lats * p.groups
    return pl.pallas_call(
        lambda *refs: contract_kernel(p, *refs),
        out_shape=shape_of((p.total * p.members * p.double, p.basis * p.kpad), BF),
        in_specs=whole(3 + p.lats),
        out_specs=pl.BlockSpec(memory_space=pltpu.VMEM),
        scratch_shapes=[
            pltpu.VMEM((p.total + 2 * HREACH, p.window, p.members * p.kpad), BF),
            pltpu.VMEM((p.total, 16, 128), F32),
            pltpu.VMEM((lines, p.wide), jnp.int32),
            pltpu.SMEM((lines, p.wide), jnp.int32),
            pltpu.SemaphoreType.DMA,
        ],
        compiler_params=params(),
        name="contract",
    )(own, far, both, *pieces)


def mix_kernel(plan, contracted, *rest):
    p = plan
    packs = rest[:4]
    keep, send, slots, mixing = rest[4:]
    a, z, x = place()
    if p.kpad > p.depth:
        for k in range(p.basis):
            mixing[k * p.kpad + p.depth : (k + 1) * p.kpad, :] = jnp.zeros(
                (p.kpad - p.depth, p.zs * p.out), BF
            )
    for ref, source in zip(packs, sources(z)):
        top = ref.shape[0] - p.fold
        for row, lane, at, column, count in folds(p):
            slots[source, at : at + count, column : column + 128] = ref[
                top + row : top + row + count, lane : lane + 128
            ]
    for b in range(p.zs):
        for k in range(p.basis):
            u, v = k // p.group, k % p.group
            mixing[k * p.kpad : k * p.kpad + p.depth, b * p.out : (b + 1) * p.out] = slots[
                b, u * p.depth : (u + 1) * p.depth, v * p.out : (v + 1) * p.out
            ]
    count = 2 * p.half
    core = lax.rem(a, 2)
    for t in range(p.ys):
        y = lax.rem(a // 2 + t, p.ys)
        for mate in range(2):
            band = 2 * y + (core if mate == 0 else 1 - core)
            at = pl.multiple_of(band * count, count)
            total = jnp.dot(
                contracted[pl.ds(at, count), :], mixing[...], preferred_element_type=F32
            ).reshape(p.cycles * p.members, 2, p.cells, p.zs * p.out)
            left = total[:, 0].reshape(p.half, p.zs * p.out)
            right = total[:, 1].reshape(p.half, p.zs * p.out)
            for w in range(2):
                value = jnp.where((x ^ w) == 0, left, right)
                if mate == 0:
                    keep[2 * t + w] = value
                else:
                    send[2 * t + w] = value.astype(BF)


def mix_basis(plan, contracted, packs):
    p = plan
    out = p.zs * p.out
    return pl.pallas_call(
        lambda *refs: mix_kernel(p, *refs),
        out_shape=[
            shape_of((2 * p.ys, p.half, out), F32),
            shape_of((2 * p.ys, p.half, out), BF),
        ],
        in_specs=whole(5),
        out_specs=whole(2),
        scratch_shapes=[
            pltpu.VMEM((p.zs, p.mix_rows, p.mix_lanes), BF),
            pltpu.VMEM((p.basis * p.kpad, out), BF),
        ],
        compiler_params=params(),
        name="mix_basis",
    )(contracted, *packs)


def add_kernel(keep, arrived, own, *msgs):
    for i in range(keep.shape[0]):
        value = keep[i] + arrived[i].astype(F32)
        if i == 0:
            own[...] = value
        else:
            msgs[i - 1][...] = value.astype(BF)


def add_cores(keep, arrived):
    count, half, out = keep.shape
    outs = pl.pallas_call(
        add_kernel,
        out_shape=[shape_of((half, out), F32)] + [shape_of((half, out), BF)] * (count - 1),
        in_specs=whole(2),
        out_specs=whole(count),
        compiler_params=params(),
        name="add_cores",
    )(keep, arrived)
    return outs[0], outs[1:]


def unpack_kernel(plan, mine, sibling, up, down, slots):
    p = plan
    a, z, x = place()
    core = lax.rem(a, 2)
    for mate, stack in enumerate((mine, sibling)):
        c = core if mate == 0 else 1 - core
        for step in range(4):
            low, high = step % 2, step // 2
            dx = jnp.where(c == 0, low, high)
            dy = jnp.where(c == 0, high, low)
            lat = 2 * ((a // 2) ^ dy) + c
            for s, source in enumerate(sources(z)):
                lon = 2 * source + (x ^ dx)
                index = step * p.zs + s
                slots[lat * p.lons + lon] = stack[index * p.out : (index + 1) * p.out, :]
    for a in range(p.lats):
        for b in range(p.lons):
            i = a * p.lons + b
            for q in range(p.lift // p.out):
                up[
                    a * p.depth + q * p.out : a * p.depth + (q + 1) * p.out,
                    b * p.lift : (b + 1) * p.lift,
                ] = slots[i, :, q * p.depth : (q + 1) * p.depth]
            down[
                b * p.out : (b + 1) * p.out, a * p.down_rows : (a + 1) * p.down_rows
            ] = slots[i, :, 2 * p.depth :]


def unpack(plan, mine, sibling):
    p = plan
    return pl.pallas_call(
        lambda *refs: unpack_kernel(p, *refs),
        out_shape=[
            shape_of((p.lats * p.depth, p.lons * p.lift), BF),
            shape_of((p.lons * p.out, p.lats * p.down_rows), BF),
        ],
        in_specs=whole(2),
        out_specs=whole(2),
        scratch_shapes=[pltpu.VMEM((p.lats * p.lons, p.out, p.mlp_lanes), BF)],
        compiler_params=params(),
        name="mlp_weights",
    )(mine, sibling)


def mlp_kernel(plan, latent, bias, up, down, own, *rest):
    p = plan
    arrived, (out, conv) = rest[:-2], rest[-2:]
    _, _, x = place()
    even = x == 0
    mine = own[...]
    other = None
    for i, ref in enumerate(arrived):
        value = ref[...].astype(F32)
        if (i + 1) % 2 == 0:
            mine = mine + value
        else:
            other = value if other is None else other + value
    first = jnp.where(even, mine, other)
    second = jnp.where(even, other, mine)
    for b in range(p.zs):
        cols = slice(b * p.out, (b + 1) * p.out)
        conv[:, 2 * b * p.out : (2 * b + 1) * p.out] = first[:, cols]
        conv[:, (2 * b + 1) * p.out : (2 * b + 2) * p.out] = second[:, cols]
    hidden = (latent[...].astype(F32).reshape(p.half, p.width) + conv[...]).astype(BF)
    lifted = jnp.dot(hidden, up[...], preferred_element_type=F32) + bias[...]
    activated = (lifted * (1.0 + lax.erf(lifted * (0.5**0.5))) * 0.5).astype(BF)
    lowered = lax.dot_general(
        activated, down[...], (((1,), (1,)), ((), ())), preferred_element_type=F32
    )
    out[...] = (hidden.astype(F32) + lowered).astype(BF).reshape(out.shape)


def mlp(plan, latent, bias, up, down, own, arrived):
    p = plan
    return pl.pallas_call(
        lambda *refs: mlp_kernel(p, *refs),
        out_shape=shape_of(latent.shape, BF),
        in_specs=whole(5 + len(arrived)),
        out_specs=pl.BlockSpec(memory_space=pltpu.VMEM),
        scratch_shapes=[pltpu.VMEM((p.half, p.width), F32)],
        compiler_params=params(),
        name="sum_mlp",
    )(latent, bias, up, down, own, *arrived)


def mover(plan):
    p = plan

    def move(value, target):
        pairs = []
        for a in range(p.lats):
            for b in range(p.lons):
                c, d = target(a, b)
                pairs.append((a * p.lons + b, (c % p.lats) * p.lons + d % p.lons))
        return lax.ppermute(value, AXES, pairs)

    return move


def after(value, *others):
    return lax.optimization_barrier((value,) + others)[0]


def shards_fast(
    plan,
    latent,
    norm_gain,
    filters,
    row_offsets,
    col_offsets,
    mix_weight,
    up_weight,
    up_bias,
    down_weight,
):
    p = plan
    move = mover(p)
    taps = filters.transpose(1, 2, 3, 0).reshape(p.cycles, p.slots * p.band, p.basis)
    msgs = normal_pieces(
        p, row_offsets.T, col_offsets.T, latent, norm_gain, taps
    )
    pieces = [msgs[0]]
    for s in range(1, p.lats):
        pieces.append(move(msgs[s], lambda i, j, s=s: (i + s, j)))
    mlp_pack, mix_pack = pack_weights(
        p, mix_weight, after(up_weight, msgs[0]), down_weight.T
    )

    def mirror(i, j):
        return i, 2 * (p.zs - 1) - 2 * (j // 2) + j % 2

    def beside(i, j):
        return i, j ^ 2

    turned = move(mix_pack, mirror)
    last = move(turned, beside)

    own = jnp.concatenate([piece[: p.body] for piece in pieces], axis=0)
    far = move(own, lambda i, j: (i, j + 2 if j % 2 else j - 2))
    both = move(jnp.concatenate([own, far], axis=0), lambda i, j: (i, j ^ 1))
    contracted = contract(p, own, far, after(both, turned), pieces)

    near = jnp.concatenate([mlp_pack, move(mlp_pack, mirror), mix_pack], axis=0)
    next_to = move(after(near, far), beside)
    packs = [mix_pack, turned, next_to, last]
    share = jnp.concatenate([near[: 2 * p.out], next_to[: 2 * p.out]], axis=0)
    share = after(share, both)
    crossed = move(share, lambda i, j: (i + 2, j) if i % 2 else (i, j ^ 1))
    share = after(jnp.concatenate([share, crossed], axis=0), turned, contracted)
    crossed = move(share, lambda i, j: (i, j ^ 1) if i % 2 else (i + 2, j))
    keep, send = mix_basis(p, contracted, packs)
    arrived = move(send, lambda i, j: (i ^ 1, j))
    mine, outgoing = add_cores(keep, arrived)
    incoming = []
    for index, value in enumerate(outgoing):
        t, w = (index + 1) // 2, (index + 1) % 2
        incoming.append(move(value, lambda i, j, t=t, w=w: (i + 2 * t, j ^ w)))

    share = after(jnp.concatenate([share, crossed], axis=0), mine)
    up, down = unpack(p, share, move(share, lambda i, j: (i ^ 1, j)))
    return mlp(p, latent, up_bias, up, down, mine, incoming)


def padded(shard, sides, width, wrap):
    for axis, dim in sides:
        size, length = (lax.axis_size(axis), shard.shape[dim])
        up = [(i, (i + 1) % size) for i in range(size if wrap else size - 1)]
        down = [(j, i) for i, j in up]
        last = lax.slice_in_dim(shard, length - width, length, axis=dim)
        leading = lax.slice_in_dim(shard, 0, width, axis=dim)
        before = lax.ppermute(last, axis, up)
        after = lax.ppermute(leading, axis, down)
        shard = jnp.concatenate([before, shard, after], axis=dim)
    return shard


def normalize(latent, norm_gain):
    widened = latent.astype(jnp.float32)
    channel_mean = jnp.mean(widened, axis=-1, keepdims=True)
    centered = widened - channel_mean
    variance = jnp.mean(centered * centered, axis=-1, keepdims=True)
    return (centered * lax.rsqrt(variance + EPSILON) * norm_gain).astype(jnp.bfloat16)


def contract_cycles(
    band_slab, filters, row_offsets, col_offsets, cycle_count, out_cells, shift_cells
):
    members = band_slab.shape[1]
    channel_share = band_slab.shape[3]

    def cycle_output(cycle_index):
        pieces = []
        for row_slot in range(R):
            where = cycle_index + HREACH + row_offsets[cycle_index, row_slot]
            source = lax.dynamic_index_in_dim(band_slab, where, 0, keepdims=False)
            start = col_offsets[cycle_index, row_slot] + shift_cells
            segment = lax.dynamic_slice_in_dim(source, start, out_cells + BW - 1, 1)
            for band_step in range(BW):
                pieces.append(segment[:, band_step : band_step + out_cells])
        stacked = jnp.stack(pieces).reshape(R * BW, members * out_cells * channel_share)
        cycle_filter = lax.dynamic_index_in_dim(filters, cycle_index, 1, keepdims=False).reshape(
            KB, R * BW
        )
        contracted = jnp.dot(cycle_filter, stacked, preferred_element_type=jnp.float32).astype(
            jnp.bfloat16
        )
        return contracted.reshape(KB, members, out_cells, channel_share)

    return lax.map(cycle_output, jnp.arange(cycle_count, dtype=jnp.int32))


def shards_plain(
    latent,
    norm_gain,
    filters,
    row_offsets,
    col_offsets,
    mix_weight,
    up_weight,
    up_bias,
    down_weight,
):
    cycle_count = latent.shape[0]
    local_cells = latent.shape[2]
    width = latent.shape[3]
    partial_weights = (
        lax.all_gather(mix_weight, "lat", axis=1, tiled=True),
        lax.all_gather(up_weight, "lat", axis=0, tiled=True),
        lax.all_gather(down_weight, "lat", axis=0, tiled=True),
    )
    mix_full, up_full, down_full = (
        lax.all_gather(partial_weights[0], "lon", axis=2, tiled=True),
        lax.all_gather(partial_weights[1], "lon", axis=1, tiled=True),
        lax.all_gather(partial_weights[2], "lon", axis=1, tiled=True),
    )
    normalized = normalize(latent, norm_gain)
    side_reach = BW // 2 + 2
    cycle_rims = padded(normalized, (("lat", 0),), HREACH, False)
    band_slab = padded(cycle_rims, (("lon", 2),), side_reach, True)
    contracted = contract_cycles(
        band_slab, filters, row_offsets, col_offsets, cycle_count, local_cells, side_reach
    )
    convolved = jnp.einsum(
        "ikejc,kcd->iejd", contracted, mix_full, preferred_element_type=jnp.float32
    )
    hidden = (latent.astype(jnp.float32) + convolved).astype(jnp.bfloat16)
    flattened = hidden.reshape(-1, width)
    lifted = jnp.dot(flattened, up_full, preferred_element_type=jnp.float32) + up_bias
    activated = jax.nn.gelu(lifted, approximate=False).astype(jnp.bfloat16)
    result = flattened.astype(jnp.float32) + jnp.dot(
        activated, down_full, preferred_element_type=jnp.float32
    )
    return result.astype(jnp.bfloat16).reshape(latent.shape)


def solution(mesh):
    lats, lons = mesh.shape["lat"], mesh.shape["lon"]

    def shards(*args):
        latent, _, filters, _, _, mix_weight, up_weight, _, down_weight = args
        plan = Plan(lats, lons, latent, filters, mix_weight, up_weight, down_weight)
        if plan.fits():
            return shards_fast(plan, *args)
        return shards_plain(*args)

    in_specs = (
        P("lat", None, "lon", None),
        P(),
        P(None, "lat", None, None),
        P("lat", None),
        P("lat", None),
        P(None, "lat", "lon"),
        P("lat", "lon"),
        P(),
        P("lat", "lon"),
    )
    out_specs = P("lat", None, "lon", None)
    return jax.shard_map(shards, mesh=mesh, in_specs=in_specs, out_specs=out_specs, check_vma=False)
```
